32 devices in a mesh: groups: 2 (over y), rows: 16 (over z, x, core).
Axes of the slice: x: 2, y: 2, z: 4, core: 2. Of those that a mesh axis runs over, the one named last changes fastest.
Arguments:
- positions: float32 [64, 2048], P('rows', 'groups'), parts along dimension 1, may hold values from -3.140625 to 3.140625
- momenta: float32 [64, 2048], P('rows', 'groups'), parts along dimension 1, may hold values from -6 to 6
- kick_strength: float32 [64, 1024], P('rows'), may hold values from 0.3 to 3
- coupling: float32 [64, 1024], P('rows'), may hold values from 0.05 to 0.5
- tangent: float32 [4, 64, 1024, 128], P('groups', 'rows'), parts along dimension 0, may hold values from -200 to 200, as said below
- log_growth: float32 [256], P('groups'), parts along dimension 0, may hold values from -4 to 4
Outputs:
- new_positions: float32 [64, 2048], P('rows', 'groups'), parts along dimension 1
- new_momenta: float32 [64, 2048], P('rows', 'groups'), parts along dimension 1
- tangent_out: float32 [4, 64, 1024, 128], P('groups', 'rows'), parts along dimension 0
- growth_out: float32 [256], P('groups'), parts along dimension 0
The draws below stay inside these ranges and needn't reach their ends.
There are 2 independent parts, one for each index of `groups`. The reference program is written for one: setup_inputs(seed, part) draws one part's arguments, and reference() takes and returns one part's arrays. A program takes and returns all parts, laid end to end along the dimension named above; an argument that names none is the same for every part. Nothing has to cross between parts.
Inputs may be any that keep to these rules, and one draw needn't show every extreme that they name: real-valued tangent vectors.
All inputs are finite; a program needn't handle non-finite values.
Results may differ from the reference program's by a relative error of at most 0.0003.
Values sent between devices are 32-bit elements; how exact they have to be, the bound alone decides.
No kernel may reach another device: no remote copies, remote signals or barrier semaphores. Data moves between devices by JAX's collectives and lax.ppermute only.
A program may use at most 64 MiB of HBM per device.

```python
import math
import jax
import jax.numpy as jnp

COLS = 1024
VECS = 128
ROWS = 64


def draw_tangent(key, part):
    key = jax.random.fold_in(key, 11)
    keys = jax.random.split(key, 4)
    history = 24
    wide_shape = (2, ROWS, COLS, VECS + history)
    column_scale = jnp.exp(jax.random.uniform(keys[1], (VECS,), jnp.float32) * math.log(4.0))
    site_scale = jnp.exp(jax.random.uniform(keys[2], (1, ROWS, COLS, 1), jnp.float32) * math.log(3.0))
    fraction = (jnp.arange(ROWS).astype(jnp.float32) / max(ROWS - 1, 1)).reshape(1, ROWS, 1, 1)
    ramp = jnp.exp(fraction * math.log(3.0))
    fresh = jnp.clip(jax.random.normal(keys[0], wide_shape, jnp.float32), -6.0, 6.0)
    common = 0.35 * jnp.clip(jax.random.normal(keys[3], (2, ROWS, COLS, 1), jnp.float32), -4.0, 4.0)
    limit = 6.0
    spread = jnp.zeros((2, ROWS, COLS, VECS), jnp.float32)
    for step in range(history + 1):
        factor = 0.8 * 0.6 ** step
        spread = spread + factor * fresh[:, :, :, history - step:history - step + VECS]
    spread = jnp.clip(spread, -limit, limit)
    base = 0.6 * spread + common
    return (base * column_scale * site_scale * ramp).astype(jnp.float32)


def level_of(own_key, shape, pieces, smallest, top_value):
    level, own = 1.0, jax.random.fold_in(own_key, 6)
    for axis_at, shards_of in pieces:
        draws = jnp.exp(jax.random.uniform(jax.random.fold_in(own, axis_at), (shards_of,), jnp.float32, smallest / len(pieces), top_value / len(pieces)))
        level = level * jnp.repeat(draws, shape[axis_at] // shards_of).reshape([-1 if axis == axis_at else 1 for axis in range(len(shape))])
    return level


def scatter_about(stream_key, dims, width, reach, pieces=(), held_as=jnp.bfloat16):
    drawn = width * jax.random.normal(stream_key, dims, jnp.float32)
    if pieces:
        drawn = drawn * level_of(stream_key, dims, pieces, -0.22, 0.18)
    return jnp.clip(drawn, -reach, reach).astype(held_as)


def setup_inputs(seed: int = 0, part: int = 0) -> dict:
    splits = jax.random.split(jax.random.key(seed), 7)
    part_keys = jax.random.split(jax.random.fold_in(splits[6], part), 7)
    positions = jnp.clip(jax.random.uniform(part_keys[0], (ROWS, COLS), jnp.float32, -3.140625, 3.140625), -3.140625, 3.140625)
    momenta = scatter_about(part_keys[1], (ROWS, COLS), 1.0, 6.0, ((0, 16),), jnp.float32)
    kick_strength = jnp.clip(jnp.exp(math.log(3.0) - 2.3025851 * jax.random.uniform(splits[2], (ROWS, COLS), jnp.float32) ** level_of(splits[2], (ROWS, COLS), ((0, 16),), -0.2, 0.2)), 0.3, 3.0)
    coupling = jnp.clip(jnp.exp(math.log(0.5) - 2.3025851 * jax.random.uniform(splits[3], (ROWS, COLS), jnp.float32) ** level_of(splits[3], (ROWS, COLS), ((0, 16),), -0.2, 0.2)), 0.05, 0.5)
    tangent = draw_tangent(jax.random.fold_in(jax.random.fold_in(splits[6], part), 71), part)
    log_growth = scatter_about(part_keys[5], (VECS,), 1.0, 4.0, (), jnp.float32)
    return {"positions": positions, "momenta": momenta, "kick_strength": kick_strength, "coupling": coupling, "tangent": tangent, "log_growth": log_growth}


def rolled(field):
    return (jnp.roll(field, 1, 0), jnp.roll(field, -1, 0), jnp.roll(field, 1, 1), jnp.roll(field, -1, 1))

def reference(positions, momenta, kick_strength, coupling, tangent, log_growth):
    angle_sides = rolled(positions)
    force = kick_strength * jnp.sin(positions)
    spring = jnp.zeros_like(positions)
    for side in angle_sides:
        spring = spring + jnp.sin(side - positions)
    new_momenta = momenta + force + coupling * spring
    new_positions = positions + new_momenta
    tan_pos = tangent[0]
    tan_mom = tangent[1]
    slope = (kick_strength * jnp.cos(positions))[:, :, None]
    tan_sides = rolled(tan_pos)
    spread = jnp.zeros_like(tan_pos)
    for side, tan_side in zip(angle_sides, tan_sides):
        weight = (coupling * jnp.cos(side - positions))[:, :, None]
        spread = spread + weight * (tan_side - tan_pos)
    mom_next = tan_mom + slope * tan_pos + spread
    pos_next = tan_pos + mom_next
    stacked = jnp.stack([pos_next, mom_next]).reshape(-1, VECS)
    ortho, upper = jnp.linalg.qr(stacked)
    diagonal = jnp.diagonal(upper)
    signs = jnp.sign(diagonal)
    sites_total = ROWS * COLS
    tangent_out = (ortho * signs[None, :] * math.sqrt(sites_total)).reshape(2, ROWS, COLS, VECS)
    growth_out = log_growth + jnp.log(jnp.abs(diagonal)) - 0.5 * math.log(sites_total)
    return (new_positions, new_momenta, tangent_out, growth_out)
```

```python
import functools
import math

import jax
import jax.numpy as jnp
from jax import lax
from jax.experimental import pallas as pl
from jax.experimental.pallas import tpu as pltpu
from jax.sharding import PartitionSpec as P

LANES = 128
MIB = 1 << 20


def lane_roll(field, shift):
    return pltpu.roll(field, shift % field.shape[1], axis=1)


def split_pair(value):
    high = value.astype(jnp.bfloat16)
    low = (value - high.astype(jnp.float32)).astype(jnp.bfloat16)
    return jnp.concatenate([high, low], axis=1)


def pair_gram(pairs):
    return lax.dot_general(
        pairs, pairs, (((0,), (0,)), ((), ())), preferred_element_type=jnp.float32
    )


def fold_pairs(gram):
    half = gram.shape[0] // 2
    return (gram[:half, :half] + gram[half:, half:]) + (gram[:half, half:] + gram[half:, :half])


def edges_kernel(tangent_ref, positions_ref, near_ref, far_ref, sems):
    rows, columns = positions_ref.shape
    odd = lax.rem(lax.axis_index("rows"), 2)
    near_row = (1 - odd) * (rows - 1)
    copies = []
    for slot, (row, out) in enumerate(((near_row, near_ref), (rows - 1 - near_row, far_ref))):
        copy = pltpu.make_async_copy(
            tangent_ref.at[0, row], out.at[pl.ds(0, columns)], sems.at[slot]
        )
        copy.start()
        copies.append(copy)
        angles = positions_ref[pl.ds(row, 1), :]
        for group in range(columns // LANES):
            out[columns + group : columns + group + 1, :] = angles[
                :, group * LANES : (group + 1) * LANES
            ]
    for copy in copies:
        copy.wait()


def inner_kernel(
    tangent_ref, positions_ref, kick_ref, coupling_ref,
    pairs_ref, partial_ref, gram_ref,
    pos_pad, mom_buf, stack, sems,
):
    rows, columns = positions_ref.shape
    groups = columns // LANES
    order = [*range(rows)]
    pos_copies = [
        pltpu.make_async_copy(
            tangent_ref.at[0, r], pos_pad.at[r, pl.ds(8, columns)], sems.at[0, r]
        )
        for r in order
    ]
    mom_copies = [
        pltpu.make_async_copy(tangent_ref.at[1, r], mom_buf.at[r], sems.at[1, r]) for r in order
    ]
    for r in order:
        pos_copies[r].start()
        mom_copies[r].start()

    x = positions_ref[...]
    coupling = coupling_ref[...]
    left = coupling * jnp.cos(lane_roll(x, 1) - x)
    right = coupling * jnp.cos(lane_roll(x, -1) - x)
    vertical = jnp.cos(x[1:] - x[:-1])
    none = jnp.zeros((1, columns), jnp.float32)
    up = coupling * jnp.concatenate([none, vertical], axis=0)
    down = coupling * jnp.concatenate([vertical, none], axis=0)
    centre = kick_ref[...] * jnp.cos(x) - ((left + right) + (up + down))
    for k, weight in enumerate((centre, left, right, up, down)):
        for r in range(rows):
            for group in range(groups):
                at = k * groups + group
                stack[r, at : at + 1, :] = weight[r : r + 1, group * LANES : (group + 1) * LANES]

    for r in order:
        pos_copies[r].wait()
        mom_copies[r].wait()
        pos_pad[r, 7:8, :] = pos_pad[r, 7 + columns : 8 + columns, :]
        pos_pad[r, 8 + columns : 9 + columns, :] = pos_pad[r, 8:9, :]

    def stepped(r, group, table, sides):
        at = 8 + group * LANES
        factor = lambda k: jnp.broadcast_to(
            table[:, k * groups + group : k * groups + group + 1], (LANES, LANES)
        )
        u = pos_pad[r, at : at + LANES, :]
        total = mom_buf[r, group * LANES : (group + 1) * LANES, :] + factor(0) * u
        total = total + factor(1) * pos_pad[r, at - 1 : at - 1 + LANES, :]
        total = total + factor(2) * pos_pad[r, at + 1 : at + 1 + LANES, :]
        for k, other in sides:
            total = total + factor(k) * pos_pad[other, at : at + LANES, :]
        return u, total

    for slot, (r, sides) in enumerate(((0, ((4, 1),)), (rows - 1, ((3, rows - 2),)))):
        table = stack[r].T
        for group in range(groups):
            _, total = stepped(r, group, table, sides)
            partial_ref[slot, group * LANES : (group + 1) * LANES, :] = total

    gram = jnp.zeros((2 * LANES, 2 * LANES), jnp.float32)
    for r in range(1, rows - 1):
        table = stack[r].T
        for group in range(groups):
            u, mom = stepped(r, group, table, ((3, r - 1), (4, r + 1)))
            span = pl.ds(group * LANES, LANES)
            pairs_ref[0, r - 1, span, :] = split_pair(u + mom)
            pairs_ref[1, r - 1, span, :] = split_pair(mom)
        for part in range(2):
            gram = gram + pair_gram(pairs_ref[part, r - 1])
    gram_ref[...] = fold_pairs(gram)


def edge_gram_kernel(
    near_ref, far_ref, partial_ref, tangent_ref, positions_ref, coupling_ref, inner_gram_ref,
    pairs_ref, gram_ref,
    pos_buf, stack, sems,
):
    rows, columns = positions_ref.shape
    groups = columns // LANES
    copies = [
        pltpu.make_async_copy(tangent_ref.at[0, r], pos_buf.at[slot], sems.at[slot])
        for slot, r in enumerate((0, rows - 1))
    ]
    for copy in copies:
        copy.start()
    odd = lax.rem(lax.axis_index("rows"), 2)
    gram = jnp.zeros((2 * LANES, 2 * LANES), jnp.float32)
    for side, received in enumerate((near_ref, far_ref)):
        slot = (1 - odd) if side == 0 else odd
        row = slot * (rows - 1)
        x = positions_ref[pl.ds(row, 1), :]
        coupling = coupling_ref[pl.ds(row, 1), :]
        for group in range(groups):
            span = slice(group * LANES, (group + 1) * LANES)
            at = side * groups + group
            stack[at : at + 1, :] = coupling[:, span] * jnp.cos(
                received[columns + group : columns + group + 1, :] - x[:, span]
            )
    for copy in copies:
        copy.wait()
    table = stack[...].T
    for side, received in enumerate((near_ref, far_ref)):
        slot = (1 - odd) if side == 0 else odd
        for group in range(groups):
            span = slice(group * LANES, (group + 1) * LANES)
            at = side * groups + group
            factor = jnp.broadcast_to(table[:, at : at + 1], (LANES, LANES))
            u = pos_buf[slot, span, :]
            mom = partial_ref[slot, span, :] + factor * (received[span, :] - u)
            pairs_ref[0, slot, span, :] = split_pair(u + mom)
            pairs_ref[1, slot, span, :] = split_pair(mom)
        for part in range(2):
            gram = gram + pair_gram(pairs_ref[part, slot])
    gram_ref[...] = inner_gram_ref[...] + fold_pairs(gram)


def inverse_factor(gram_ref, inverse_ref):
    order = gram_ref.shape[0]
    step = 8
    lane = lax.broadcasted_iota(jnp.int32, (step, order), 1)
    sub = lax.broadcasted_iota(jnp.int32, (step, order), 0)
    spread = lambda value: jnp.broadcast_to(value, (step, order))
    work = [gram_ref[at : at + step, :] for at in range(0, order, step)]
    squares = jnp.ones((step, order), jnp.float32)
    for block in range(order // step):
        first = block * step
        own = work[block]
        columns = [spread(own[:, first + a : first + a + 1]) for a in range(step)]
        pivot = [
            [spread(columns[a][i : i + 1, :]) if i >= a else None for a in range(step)]
            for i in range(step)
        ]
        inside = (lane >= first) & (lane < first + step)
        extended = jnp.where(inside, jnp.where(lane - first == sub, 1.0, 0.0), own)
        solved = [spread(extended[a : a + 1, :]) for a in range(step)]
        recip = [None] * step
        lower = [[None] * step for _ in range(step)]
        for a in range(step):
            recip[a] = 1.0 / pivot[a][a]
            for i in range(a + 1, step):
                lower[i][a] = pivot[i][a] * recip[a]
            for b in range(a + 1, step):
                for i in range(b, step):
                    pivot[i][b] = pivot[i][b] - lower[i][a] * pivot[b][a]
        for a in range(step):
            for i in range(a + 1, step):
                solved[i] = solved[i] - lower[i][a] * solved[a]
        scaled = [solved[a] * recip[a] for a in range(step)]
        for a in range(step - 1, 0, -1):
            for i in range(a):
                scaled[i] = scaled[i] - lower[a][i] * scaled[a]
        for later in range(block + 1, order // step):
            rest = work[later]
            t = [spread(rest[:, first + a : first + a + 1]) * scaled[a] for a in range(step)]
            while len(t) > 1:
                t = [t[i] + t[i + 1] for i in range(0, len(t), 2)]
            work[later] = jnp.where(inside, 0.0, rest) - t[0]
        rows_out, diagonal = solved[0], pivot[0][0]
        for a in range(step):
            rows_out = jnp.where(sub == a, solved[a], rows_out)
            diagonal = jnp.where(sub == a, pivot[a][a], diagonal)
            squares = jnp.where(lane == first + a, pivot[a][a], squares)
        inverse_ref[first : first + step, :] = jnp.where(
            lane <= first + sub, rows_out * lax.rsqrt(diagonal), 0.0
        )
    return squares


def ortho_kernel(
    sites_total, gram_ref, log_growth_ref, inner_ref, edge_ref,
    out_ref, growth_ref,
    inverse_ref, inner_buf, edge_buf, out_buf, in_sems, out_sems,
):
    rows = out_ref.shape[1]
    loads = [
        pltpu.make_async_copy(inner_ref, inner_buf, in_sems.at[0]),
        pltpu.make_async_copy(edge_ref, edge_buf, in_sems.at[1]),
    ]
    for load in loads:
        load.start()
    squares = inverse_factor(gram_ref, inverse_ref)
    growth_ref[...] = (
        log_growth_ref[...] + 0.5 * jnp.log(squares[:1]) - 0.5 * math.log(sites_total)
    )
    factor = split_pair(inverse_ref[...] * math.sqrt(sites_total))
    high, low = factor[:, :LANES], factor[:, LANES:]
    weights = jnp.concatenate(
        [jnp.concatenate([high, high], axis=1), jnp.concatenate([low, low], axis=1)], axis=0
    )
    for load in loads:
        load.wait()
    stores = []
    for part in range(2):
        for r in range(rows):
            if r in (0, rows - 1):
                pairs = edge_buf[part, 0 if r == 0 else 1]
            else:
                pairs = inner_buf[part, r - 1]
            both = lax.dot_general(
                pairs, weights, (((1,), (1,)), ((), ())), preferred_element_type=jnp.float32
            )
            out_buf[part, r] = both[:, :LANES] + both[:, LANES:]
            store = pltpu.make_async_copy(
                out_buf.at[part, r], out_ref.at[part, r], out_sems.at[part, r]
            )
            store.start()
            stores.append(store)
    for store in stores:
        store.wait()


def sum_over_rows(value):
    devices = lax.axis_size("rows")
    if devices & (devices - 1):
        return lax.psum(value, "rows")
    bit = 1
    while bit < devices:
        value = value + lax.ppermute(value, "rows", [(i, i ^ bit) for i in range(devices)])
        bit *= 2
    return value


def local(positions, momenta, kick_strength, coupling, tangent, log_growth):
    rows, columns = positions.shape
    vectors = tangent.shape[3]
    devices = lax.axis_size("rows")
    groups = columns // LANES
    anywhere = pl.BlockSpec(memory_space=pl.ANY)
    resident = pl.BlockSpec(memory_space=pltpu.VMEM)
    f32 = lambda *shape: jax.ShapeDtypeStruct(shape, jnp.float32)
    bf16 = lambda *shape: jax.ShapeDtypeStruct(shape, jnp.bfloat16)

    near, far = pl.pallas_call(
        edges_kernel,
        out_shape=[f32(columns + groups, vectors)] * 2,
        in_specs=[anywhere, resident],
        out_specs=[resident] * 2,
        scratch_shapes=[pltpu.SemaphoreType.DMA((2,))],
        name="edges",
    )(tangent, positions)
    far = lax.ppermute(
        far, "rows", [(i, (i + 1 if i % 2 else i - 1) % devices) for i in range(devices)]
    )
    near = lax.ppermute(near, "rows", [(i, i ^ 1) for i in range(devices)])

    inner_pairs, partial, inner_gram = pl.pallas_call(
        inner_kernel,
        out_shape=[
            bf16(2, rows - 2, columns, 2 * vectors),
            f32(2, columns, vectors),
            f32(vectors, vectors),
        ],
        in_specs=[anywhere, resident, resident, resident],
        out_specs=[resident] * 3,
        scratch_shapes=[
            pltpu.VMEM((rows, columns + 16, vectors), jnp.float32),
            pltpu.VMEM((rows, columns, vectors), jnp.float32),
            pltpu.VMEM((rows, LANES, LANES), jnp.float32),
            pltpu.SemaphoreType.DMA((2, rows)),
        ],
        compiler_params=pltpu.CompilerParams(vmem_limit_bytes=24 * MIB),
        cost_estimate=pl.CostEstimate(
            flops=2 * 10**9, bytes_accessed=8 * MIB, transcendentals=0
        ),
        name="inner",
    )(tangent, positions, kick_strength, coupling)

    edge_pairs, gram = pl.pallas_call(
        edge_gram_kernel,
        out_shape=[bf16(2, 2, columns, 2 * vectors), f32(vectors, vectors)],
        in_specs=[resident, resident, resident, anywhere, resident, resident, resident],
        out_specs=[resident] * 2,
        scratch_shapes=[
            pltpu.VMEM((2, columns, vectors), jnp.float32),
            pltpu.VMEM((LANES, LANES), jnp.float32),
            pltpu.SemaphoreType.DMA((2,)),
        ],
        compiler_params=pltpu.CompilerParams(vmem_limit_bytes=16 * MIB),
        name="edge_gram",
    )(near, far, partial, tangent, positions, coupling, inner_gram)
    gram = sum_over_rows(gram)

    near_angles = near[columns:].reshape(1, columns)
    far_angles = far[columns:].reshape(1, columns)
    odd = lax.axis_index("rows") % 2 == 1
    above = jnp.where(odd, near_angles, far_angles)
    below = jnp.where(odd, far_angles, near_angles)
    padded = jnp.concatenate([above, positions, below], axis=0)
    spring = jnp.sin(padded[:-2] - positions) + jnp.sin(padded[2:] - positions)
    spring = spring + jnp.sin(jnp.roll(positions, 1, 1) - positions)
    spring = spring + jnp.sin(jnp.roll(positions, -1, 1) - positions)
    new_momenta = momenta + kick_strength * jnp.sin(positions) + coupling * spring
    new_positions = positions + new_momenta

    sites_total = rows * devices * columns
    tangent_out, growth = pl.pallas_call(
        functools.partial(ortho_kernel, sites_total),
        out_shape=[f32(2, rows, columns, vectors), f32(1, vectors)],
        in_specs=[resident, resident, anywhere, anywhere],
        out_specs=[anywhere, resident],
        scratch_shapes=[
            pltpu.VMEM((vectors, vectors), jnp.float32),
            pltpu.VMEM((2, rows - 2, columns, 2 * vectors), jnp.bfloat16),
            pltpu.VMEM((2, 2, columns, 2 * vectors), jnp.bfloat16),
            pltpu.VMEM((2, rows, columns, vectors), jnp.float32),
            pltpu.SemaphoreType.DMA((2,)),
            pltpu.SemaphoreType.DMA((2, rows)),
        ],
        compiler_params=pltpu.CompilerParams(vmem_limit_bytes=24 * MIB),
        name="ortho",
    )(gram, log_growth.reshape(1, vectors), inner_pairs, edge_pairs)
    return (new_positions, new_momenta, tangent_out, growth.reshape(vectors))


def solution(mesh):
    placed = (
        P("rows", "groups"),
        P("rows", "groups"),
        P("rows", None),
        P("rows", None),
        P("groups", "rows", None, None),
        P("groups"),
    )
    return jax.shard_map(
        local,
        mesh=mesh,
        in_specs=placed,
        out_specs=(
            P("rows", "groups"),
            P("rows", "groups"),
            P("groups", "rows", None, None),
            P("groups"),
        ),
        check_vma=False,
    )
```

```python
import functools
import math

import jax
import jax.numpy as jnp
from jax import lax
from jax.experimental import pallas as pl
from jax.experimental.pallas import tpu as pltpu
from jax.sharding import PartitionSpec as P

LANES = 128
MIB = 1 << 20


def lane_roll(field, shift):
    return pltpu.roll(field, shift % field.shape[1], axis=1)


def split_pair(value):
    high = value.astype(jnp.bfloat16)
    low = (value - high.astype(jnp.float32)).astype(jnp.bfloat16)
    return jnp.concatenate([high, low], axis=1)


def pair_gram(pairs):
    return lax.dot_general(
        pairs, pairs, (((0,), (0,)), ((), ())), preferred_element_type=jnp.float32
    )


def fold_pairs(gram):
    half = gram.shape[0] // 2
    return (gram[:half, :half] + gram[half:, half:]) + (gram[:half, half:] + gram[half:, :half])


def edges_kernel(
    tangent_ref, positions_hbm, near_ref, far_ref, tail_ref, positions_ref, sems
):
    rows, columns = positions_ref.shape
    head = columns - tail_ref.shape[0]
    odd = lax.rem(lax.axis_index("rows"), 2)
    near_row = (1 - odd) * (rows - 1)
    far_row = rows - 1 - near_row
    near, far = tangent_ref.at[0, near_row], tangent_ref.at[0, far_row]
    copies = [
        pltpu.make_async_copy(far.at[pl.ds(0, head)], far_ref.at[pl.ds(0, head)], sems.at[0]),
        pltpu.make_async_copy(far.at[pl.ds(head, columns - head)], tail_ref, sems.at[1]),
        pltpu.make_async_copy(near, near_ref.at[pl.ds(0, columns)], sems.at[2]),
    ]
    angle_copy = pltpu.make_async_copy(positions_hbm, positions_ref, sems.at[3])
    angle_copy.start()
    for copy in copies:
        copy.start()
    angle_copy.wait()
    for row, at, out in ((near_row, columns, near_ref), (far_row, head, far_ref)):
        angles = positions_ref[pl.ds(row, 1), :]
        for group in range(columns // LANES):
            out[at + group : at + group + 1, :] = angles[:, group * LANES : (group + 1) * LANES]
    for copy in copies:
        copy.wait()


def inner_kernel(
    tangent_ref, positions_ref, kick_ref, coupling_ref,
    pairs_ref, partial_ref, gram_ref,
    pos_pad, mom_buf, stack, sems,
):
    rows, columns = positions_ref.shape
    groups = columns // LANES
    order = [*range(rows)]
    pos_copies = [
        pltpu.make_async_copy(
            tangent_ref.at[0, r], pos_pad.at[r, pl.ds(8, columns)], sems.at[0, r]
        )
        for r in order
    ]
    mom_copies = [
        pltpu.make_async_copy(tangent_ref.at[1, r], mom_buf.at[r], sems.at[1, r]) for r in order
    ]
    for r in order:
        pos_copies[r].start()
        mom_copies[r].start()

    x = positions_ref[...]
    coupling = coupling_ref[...]
    left = coupling * jnp.cos(lane_roll(x, 1) - x)
    right = coupling * jnp.cos(lane_roll(x, -1) - x)
    vertical = jnp.cos(x[1:] - x[:-1])
    none = jnp.zeros((1, columns), jnp.float32)
    up = coupling * jnp.concatenate([none, vertical], axis=0)
    down = coupling * jnp.concatenate([vertical, none], axis=0)
    centre = kick_ref[...] * jnp.cos(x) - ((left + right) + (up + down))
    for k, weight in enumerate((centre, left, right, up, down)):
        for r in range(rows):
            for group in range(groups):
                at = k * groups + group
                stack[r, at : at + 1, :] = weight[r : r + 1, group * LANES : (group + 1) * LANES]

    for r in order:
        pos_copies[r].wait()
        mom_copies[r].wait()
        pos_pad[r, 7:8, :] = pos_pad[r, 7 + columns : 8 + columns, :]
        pos_pad[r, 8 + columns : 9 + columns, :] = pos_pad[r, 8:9, :]

    def stepped(r, group, table, sides):
        at = 8 + group * LANES
        factor = lambda k: jnp.broadcast_to(
            table[:, k * groups + group : k * groups + group + 1], (LANES, LANES)
        )
        u = pos_pad[r, at : at + LANES, :]
        total = mom_buf[r, group * LANES : (group + 1) * LANES, :] + factor(0) * u
        total = total + factor(1) * pos_pad[r, at - 1 : at - 1 + LANES, :]
        total = total + factor(2) * pos_pad[r, at + 1 : at + 1 + LANES, :]
        for k, other in sides:
            total = total + factor(k) * pos_pad[other, at : at + LANES, :]
        return u, total

    for slot, (r, sides) in enumerate(((0, ((4, 1),)), (rows - 1, ((3, rows - 2),)))):
        table = stack[r].T
        for group in range(groups):
            u, total = stepped(r, group, table, sides)
            partial_ref[0, slot, group * LANES : (group + 1) * LANES, :] = u
            partial_ref[1, slot, group * LANES : (group + 1) * LANES, :] = total

    gram = jnp.zeros((2 * LANES, 2 * LANES), jnp.float32)
    for r in range(1, rows - 1):
        table = stack[r].T
        for group in range(groups):
            u, mom = stepped(r, group, table, ((3, r - 1), (4, r + 1)))
            span = pl.ds(group * LANES, LANES)
            pairs_ref[0, r - 1, span, :] = split_pair(u + mom)
            pairs_ref[1, r - 1, span, :] = split_pair(mom)
        for part in range(2):
            gram = gram + pair_gram(pairs_ref[part, r - 1])
    gram_ref[...] = fold_pairs(gram)


def side_slot(side):
    odd = lax.rem(lax.axis_index("rows"), 2)
    return odd if side else 1 - odd


def row_gram_kernel(
    side, first, angles_at, angles_ref, halo_ref, partial_ref, positions_ref, coupling_ref,
    before_ref, pairs_ref, gram_ref, stack,
):
    columns = positions_ref.shape[1]
    sites = pairs_ref.shape[1]
    slot = side_slot(side)
    row = slot * (positions_ref.shape[0] - 1)
    x = positions_ref[pl.ds(row, 1), :]
    coupling = coupling_ref[pl.ds(row, 1), :]
    for group in range(sites // LANES):
        span = slice(first + group * LANES, first + (group + 1) * LANES)
        at = angles_at + first // LANES + group
        stack[group : group + 1, :] = coupling[:, span] * jnp.cos(
            angles_ref[at : at + 1, :] - x[:, span]
        )
    table = stack[...].T
    for group in range(sites // LANES):
        span = slice(group * LANES, (group + 1) * LANES)
        from_first = slice(first + group * LANES, first + (group + 1) * LANES)
        factor = jnp.broadcast_to(table[:, group : group + 1], (LANES, LANES))
        u = partial_ref[0, slot, from_first, :]
        mom = partial_ref[1, slot, from_first, :] + factor * (halo_ref[span, :] - u)
        pairs_ref[0, span, :] = split_pair(u + mom)
        pairs_ref[1, span, :] = split_pair(mom)
    gram = pair_gram(pairs_ref[0]) + pair_gram(pairs_ref[1])
    gram_ref[...] = before_ref[...] + fold_pairs(gram)


def add_kernel(left_ref, right_ref, out_ref):
    out_ref[...] = left_ref[...] + right_ref[...]


def angles_kernel(
    near_at, far_at, near_ref, far_ref, positions_ref, momenta_ref, kick_ref, coupling_ref,
    new_positions_ref, new_momenta_ref,
):
    rows, columns = positions_ref.shape
    odd = lax.rem(lax.axis_index("rows"), 2) == 1
    lay = lambda ref, at: jnp.concatenate(
        [ref[at + g : at + g + 1, :] for g in range(columns // LANES)], axis=1
    )
    near, far = lay(near_ref, near_at), lay(far_ref, far_at)
    x = positions_ref[...]
    above = jnp.concatenate([jnp.where(odd, near, far), x[:-1]], axis=0)
    below = jnp.concatenate([x[1:], jnp.where(odd, far, near)], axis=0)
    spring = jnp.sin(above - x) + jnp.sin(below - x)
    spring = spring + jnp.sin(lane_roll(x, 1) - x)
    spring = spring + jnp.sin(lane_roll(x, -1) - x)
    momenta = momenta_ref[...] + kick_ref[...] * jnp.sin(x) + coupling_ref[...] * spring
    new_momenta_ref[...] = momenta
    new_positions_ref[...] = x + momenta


def inverse_factor(gram, inverse_ref):
    order = gram.shape[0]
    step = 8
    lane = lax.broadcasted_iota(jnp.int32, (step, order), 1)
    sub = lax.broadcasted_iota(jnp.int32, (step, order), 0)
    spread = lambda value: jnp.broadcast_to(value, (step, order))
    work = [gram[at : at + step, :] for at in range(0, order, step)]
    squares = jnp.ones((step, order), jnp.float32)
    for block in range(order // step):
        first = block * step
        own = work[block]
        columns = [spread(own[:, first + a : first + a + 1]) for a in range(step)]
        pivot = [
            [spread(columns[a][i : i + 1, :]) if i >= a else None for a in range(step)]
            for i in range(step)
        ]
        inside = (lane >= first) & (lane < first + step)
        extended = jnp.where(inside, jnp.where(lane - first == sub, 1.0, 0.0), own)
        solved = [spread(extended[a : a + 1, :]) for a in range(step)]
        recip = [None] * step
        lower = [[None] * step for _ in range(step)]
        for a in range(step):
            recip[a] = 1.0 / pivot[a][a]
            for i in range(a + 1, step):
                lower[i][a] = pivot[i][a] * recip[a]
            for b in range(a + 1, step):
                for i in range(b, step):
                    pivot[i][b] = pivot[i][b] - lower[i][a] * pivot[b][a]
        for a in range(step):
            for i in range(a + 1, step):
                solved[i] = solved[i] - lower[i][a] * solved[a]
        scaled = [solved[a] * recip[a] for a in range(step)]
        for a in range(step - 1, 0, -1):
            for i in range(a):
                scaled[i] = scaled[i] - lower[a][i] * scaled[a]
        for later in range(block + 1, order // step):
            rest = work[later]
            t = [spread(rest[:, first + a : first + a + 1]) * scaled[a] for a in range(step)]
            while len(t) > 1:
                t = [t[i] + t[i + 1] for i in range(0, len(t), 2)]
            work[later] = jnp.where(inside, 0.0, rest) - t[0]
        rows_out, diagonal = solved[0], pivot[0][0]
        for a in range(step):
            rows_out = jnp.where(sub == a, solved[a], rows_out)
            diagonal = jnp.where(sub == a, pivot[a][a], diagonal)
            squares = jnp.where(lane == first + a, pivot[a][a], squares)
        inverse_ref[first : first + step, :] = jnp.where(
            lane <= first + sub, rows_out * lax.rsqrt(diagonal), 0.0
        )
    return squares


def ortho_kernel(
    sites_total, gram_ref, other_ref, log_growth_ref, inner_ref, near_ref, far_ref, tail_ref,
    out_ref, growth_ref,
    inverse_ref, out_buf, out_sems,
):
    rows, columns = out_ref.shape[1], out_ref.shape[2]
    head = far_ref.shape[1]
    squares = inverse_factor(gram_ref[...] + other_ref[...], inverse_ref)
    growth_ref[...] = (
        log_growth_ref[...] + 0.5 * jnp.log(squares[:1]) - 0.5 * math.log(sites_total)
    )
    factor = split_pair(inverse_ref[...] * math.sqrt(sites_total))
    high, low = factor[:, :LANES], factor[:, LANES:]
    weights = jnp.concatenate(
        [jnp.concatenate([high, high], axis=1), jnp.concatenate([low, low], axis=1)], axis=0
    )

    def product(pairs):
        both = lax.dot_general(
            pairs, weights, (((1,), (1,)), ((), ())), preferred_element_type=jnp.float32
        )
        return both[:, :LANES] + both[:, LANES:]

    stores = []

    def send(part, slot, row):
        store = pltpu.make_async_copy(
            out_buf.at[part, slot], out_ref.at[part, row], out_sems.at[part, slot]
        )
        store.start()
        stores.append(store)

    for part in range(2):
        for r in range(rows - 2):
            out_buf[part, r] = product(inner_ref[part, r])
            send(part, r, r + 1)
        out_buf[part, rows - 2] = product(near_ref[part])
        send(part, rows - 2, side_slot(0) * (rows - 1))
        out_buf[part, rows - 1, :head] = product(far_ref[part])
        out_buf[part, rows - 1, head:] = product(tail_ref[part])
        send(part, rows - 1, side_slot(1) * (rows - 1))
    for store in stores:
        store.wait()


def sum_over_rows(value, summed):
    devices = lax.axis_size("rows")
    if devices & (devices - 1):
        return lax.psum(value, "rows"), jnp.zeros_like(value)
    bit, other = 1, None
    while bit < devices:
        if other is not None:
            value = summed(value, other)
        other = lax.ppermute(value, "rows", [(i, i ^ bit) for i in range(devices)])
        bit *= 2
    return value, other


def local(positions, momenta, kick_strength, coupling, tangent, log_growth):
    rows, columns = positions.shape
    vectors = tangent.shape[3]
    devices = lax.axis_size("rows")
    groups = columns // LANES
    in_hbm = pl.BlockSpec(memory_space=pltpu.HBM)
    resident = pl.BlockSpec(memory_space=pltpu.VMEM)
    f32 = lambda *shape: pltpu.VMEM(shape, jnp.float32)
    bf16 = lambda *shape: pltpu.VMEM(shape, jnp.bfloat16)
    near_core = lambda array: pltpu.with_memory_space_constraint(array, pltpu.VMEM)
    tangent = pltpu.with_memory_space_constraint(tangent, pltpu.HBM)

    tail_sites = columns // 4 if columns % (4 * LANES) == 0 else LANES
    head = columns - tail_sites
    near, far, tail = pl.pallas_call(
        edges_kernel,
        out_shape=[
            f32(columns + groups, vectors), f32(head + groups, vectors), f32(tail_sites, vectors)
        ],
        in_specs=[in_hbm, in_hbm],
        out_specs=[resident] * 3,
        scratch_shapes=[
            pltpu.VMEM((rows, columns), jnp.float32), pltpu.SemaphoreType.DMA((4,))
        ],
        compiler_params=pltpu.CompilerParams(vmem_limit_bytes=4 * MIB),
        name="edges",
    )(tangent, pltpu.with_memory_space_constraint(positions, pltpu.HBM))
    outward = [(i, (i + 1 if i % 2 else i - 1) % devices) for i in range(devices)]
    far = lax.ppermute(far, "rows", outward)
    near = lax.ppermute(near, "rows", [(i, i ^ 1) for i in range(devices)])
    tail = lax.ppermute(tail, "rows", outward)

    inner_pairs, partial, inner_gram = pl.pallas_call(
        inner_kernel,
        out_shape=[
            bf16(2, rows - 2, columns, 2 * vectors),
            f32(2, 2, columns, vectors),
            f32(vectors, vectors),
        ],
        in_specs=[in_hbm, resident, resident, resident],
        out_specs=[resident] * 3,
        scratch_shapes=[
            pltpu.VMEM((rows, columns + 16, vectors), jnp.float32),
            pltpu.VMEM((rows, columns, vectors), jnp.float32),
            pltpu.VMEM((rows, LANES, LANES), jnp.float32),
            pltpu.SemaphoreType.DMA((2, rows)),
        ],
        compiler_params=pltpu.CompilerParams(vmem_limit_bytes=16 * MIB),
        cost_estimate=pl.CostEstimate(
            flops=2 * 10**9, bytes_accessed=8 * MIB, transcendentals=0
        ),
        name="inner",
    )(tangent, positions, kick_strength, coupling)

    def finish(name, side, first, sites, angles_at, angles, halo, before):
        return pl.pallas_call(
            functools.partial(row_gram_kernel, side, first, angles_at),
            out_shape=[bf16(2, sites, 2 * vectors), f32(vectors, vectors)],
            in_specs=[resident] * 6,
            out_specs=[resident] * 2,
            scratch_shapes=[pltpu.VMEM((LANES, LANES), jnp.float32)],
            compiler_params=pltpu.CompilerParams(vmem_limit_bytes=8 * MIB),
            cost_estimate=pl.CostEstimate(
                flops=4 * 10**8, bytes_accessed=2 * MIB, transcendentals=0
            ),
            name=name,
        )(
            near_core(angles), near_core(halo), near_core(partial), near_core(positions),
            near_core(coupling), near_core(before),
        )

    near_pairs, gram = finish("near", 0, 0, columns, columns, near, near, inner_gram)
    far_pairs, gram = finish("far", 1, 0, head, head, far, far, gram)
    tail_pairs, gram = finish("tail", 1, head, tail_sites, head, far, tail, gram)

    def summed(left, right):
        return pl.pallas_call(
            add_kernel,
            out_shape=f32(vectors, vectors),
            in_specs=[resident] * 2,
            out_specs=resident,
            compiler_params=pltpu.CompilerParams(vmem_limit_bytes=1 * MIB),
            name="gram_sum",
        )(near_core(left), near_core(right))

    gram, gram_other = sum_over_rows(gram, summed)

    new_positions, new_momenta = pl.pallas_call(
        functools.partial(angles_kernel, columns, head),
        out_shape=[jax.ShapeDtypeStruct((rows, columns), jnp.float32)] * 2,
        in_specs=[resident] * 6,
        out_specs=[resident] * 2,
        compiler_params=pltpu.CompilerParams(vmem_limit_bytes=4 * MIB),
        cost_estimate=pl.CostEstimate(flops=10**6, bytes_accessed=10**6, transcendentals=0),
        name="angles",
    )(near_core(near), near_core(far), positions, momenta, kick_strength, coupling)

    sites_total = rows * devices * columns
    tangent_out, growth = pl.pallas_call(
        functools.partial(ortho_kernel, sites_total),
        out_shape=[
            pltpu.HBM((2, rows, columns, vectors), jnp.float32),
            jax.ShapeDtypeStruct((1, vectors), jnp.float32),
        ],
        in_specs=[resident] * 7,
        out_specs=[in_hbm, resident],
        scratch_shapes=[
            pltpu.VMEM((vectors, vectors), jnp.float32),
            pltpu.VMEM((2, rows, columns, vectors), jnp.float32),
            pltpu.SemaphoreType.DMA((2, rows)),
        ],
        compiler_params=pltpu.CompilerParams(vmem_limit_bytes=16 * MIB),
        name="ortho",
    )(
        near_core(gram), near_core(gram_other), log_growth.reshape(1, vectors),
        near_core(inner_pairs), near_core(near_pairs), near_core(far_pairs), near_core(tail_pairs),
    )
    return (new_positions, new_momenta, tangent_out, growth.reshape(vectors))


def solution(mesh):
    placed = (
        P("rows", "groups"),
        P("rows", "groups"),
        P("rows", None),
        P("rows", None),
        P("groups", "rows", None, None),
        P("groups"),
    )
    return jax.shard_map(
        local,
        mesh=mesh,
        in_specs=placed,
        out_specs=(
            P("rows", "groups"),
            P("rows", "groups"),
            P("groups", "rows", None, None),
            P("groups"),
        ),
        check_vma=False,
    )
```

```python
import functools
import math

import jax
import jax.numpy as jnp
from jax import lax
from jax.experimental import pallas as pl
from jax.experimental.pallas import tpu as pltpu
from jax.sharding import PartitionSpec as P

LANES = 128
MIB = 1 << 20


def lane_roll(field, shift):
    return pltpu.roll(field, shift % field.shape[1], axis=1)


def split_pair(value):
    high = value.astype(jnp.bfloat16)
    low = (value - high.astype(jnp.float32)).astype(jnp.bfloat16)
    return jnp.concatenate([high, low], axis=1)


def pair_gram(pairs):
    return lax.dot_general(
        pairs, pairs, (((0,), (0,)), ((), ())), preferred_element_type=jnp.float32
    )


def fold_pairs(gram):
    half = gram.shape[0] // 2
    return (gram[:half, :half] + gram[half:, half:]) + (gram[:half, half:] + gram[half:, :half])


def edges_kernel(
    tangent_ref, positions_hbm, near_ref, far_ref, tail_ref, positions_ref, sems
):
    rows, columns = positions_ref.shape
    head = columns - tail_ref.shape[0]
    odd = lax.rem(lax.axis_index("rows"), 2)
    near_row = (1 - odd) * (rows - 1)
    far_row = rows - 1 - near_row
    near, far = tangent_ref.at[0, near_row], tangent_ref.at[0, far_row]
    copies = [
        pltpu.make_async_copy(far.at[pl.ds(0, head)], far_ref.at[pl.ds(0, head)], sems.at[0]),
        pltpu.make_async_copy(far.at[pl.ds(head, columns - head)], tail_ref, sems.at[1]),
        pltpu.make_async_copy(near, near_ref.at[pl.ds(0, columns)], sems.at[2]),
    ]
    angle_copy = pltpu.make_async_copy(positions_hbm, positions_ref, sems.at[3])
    angle_copy.start()
    for copy in copies:
        copy.start()
    angle_copy.wait()
    for row, at, out in ((near_row, columns, near_ref), (far_row, head, far_ref)):
        angles = positions_ref[pl.ds(row, 1), :]
        for group in range(columns // LANES):
            out[at + group : at + group + 1, :] = angles[:, group * LANES : (group + 1) * LANES]
    for copy in copies:
        copy.wait()


def inner_kernel(
    tangent_ref, positions_ref, kick_ref, coupling_ref,
    pairs_ref, partial_ref, gram_ref,
    pos_pad, mom_buf, stack, sems,
):
    rows, columns = positions_ref.shape
    groups = columns // LANES
    order = [*range(rows)]
    pos_copies = [
        pltpu.make_async_copy(
            tangent_ref.at[0, r], pos_pad.at[r, pl.ds(8, columns)], sems.at[0, r]
        )
        for r in order
    ]
    mom_copies = [
        pltpu.make_async_copy(tangent_ref.at[1, r], mom_buf.at[r], sems.at[1, r]) for r in order
    ]
    for r in order:
        pos_copies[r].start()
        mom_copies[r].start()

    x = positions_ref[...]
    coupling = coupling_ref[...]
    left = coupling * jnp.cos(lane_roll(x, 1) - x)
    right = coupling * jnp.cos(lane_roll(x, -1) - x)
    vertical = jnp.cos(x[1:] - x[:-1])
    none = jnp.zeros((1, columns), jnp.float32)
    up = coupling * jnp.concatenate([none, vertical], axis=0)
    down = coupling * jnp.concatenate([vertical, none], axis=0)
    centre = kick_ref[...] * jnp.cos(x) - ((left + right) + (up + down))
    for k, weight in enumerate((centre, left, right, up, down)):
        for r in range(rows):
            for group in range(groups):
                at = k * groups + group
                stack[r, at : at + 1, :] = weight[r : r + 1, group * LANES : (group + 1) * LANES]

    for r in order:
        pos_copies[r].wait()
        mom_copies[r].wait()
        pos_pad[r, 7:8, :] = pos_pad[r, 7 + columns : 8 + columns, :]
        pos_pad[r, 8 + columns : 9 + columns, :] = pos_pad[r, 8:9, :]

    def stepped(r, group, table, sides):
        at = 8 + group * LANES
        factor = lambda k: jnp.broadcast_to(
            table[:, k * groups + group : k * groups + group + 1], (LANES, LANES)
        )
        u = pos_pad[r, at : at + LANES, :]
        total = mom_buf[r, group * LANES : (group + 1) * LANES, :] + factor(0) * u
        total = total + factor(1) * pos_pad[r, at - 1 : at - 1 + LANES, :]
        total = total + factor(2) * pos_pad[r, at + 1 : at + 1 + LANES, :]
        for k, other in sides:
            total = total + factor(k) * pos_pad[other, at : at + LANES, :]
        return u, total

    for slot, (r, sides) in enumerate(((0, ((4, 1),)), (rows - 1, ((3, rows - 2),)))):
        table = stack[r].T
        for group in range(groups):
            u, total = stepped(r, group, table, sides)
            partial_ref[0, slot, group * LANES : (group + 1) * LANES, :] = u
            partial_ref[1, slot, group * LANES : (group + 1) * LANES, :] = total

    gram = jnp.zeros((2 * LANES, 2 * LANES), jnp.float32)
    for r in range(1, rows - 1):
        table = stack[r].T
        for group in range(groups):
            u, mom = stepped(r, group, table, ((3, r - 1), (4, r + 1)))
            span = pl.ds(group * LANES, LANES)
            pairs_ref[0, r - 1, span, :] = split_pair(u + mom)
            pairs_ref[1, r - 1, span, :] = split_pair(mom)
        for part in range(2):
            gram = gram + pair_gram(pairs_ref[part, r - 1])
    gram_ref[...] = fold_pairs(gram)


def side_slot(side):
    odd = lax.rem(lax.axis_index("rows"), 2)
    return odd if side else 1 - odd


def row_gram_kernel(
    side, first, angles_at, angles_ref, halo_ref, partial_ref, positions_ref, coupling_ref,
    before_ref, pairs_ref, gram_ref, stack,
):
    columns = positions_ref.shape[1]
    sites = pairs_ref.shape[1]
    slot = side_slot(side)
    row = slot * (positions_ref.shape[0] - 1)
    x = positions_ref[pl.ds(row, 1), :]
    coupling = coupling_ref[pl.ds(row, 1), :]
    for group in range(sites // LANES):
        span = slice(first + group * LANES, first + (group + 1) * LANES)
        at = angles_at + first // LANES + group
        stack[group : group + 1, :] = coupling[:, span] * jnp.cos(
            angles_ref[at : at + 1, :] - x[:, span]
        )
    table = stack[...].T
    for group in range(sites // LANES):
        span = slice(group * LANES, (group + 1) * LANES)
        from_first = slice(first + group * LANES, first + (group + 1) * LANES)
        factor = jnp.broadcast_to(table[:, group : group + 1], (LANES, LANES))
        u = partial_ref[0, slot, from_first, :]
        mom = partial_ref[1, slot, from_first, :] + factor * (halo_ref[span, :] - u)
        pairs_ref[0, span, :] = split_pair(u + mom)
        pairs_ref[1, span, :] = split_pair(mom)
    gram = pair_gram(pairs_ref[0]) + pair_gram(pairs_ref[1])
    gram_ref[...] = before_ref[...] + fold_pairs(gram)


def add_kernel(left_ref, right_ref, out_ref):
    out_ref[...] = left_ref[...] + right_ref[...]


def angles_kernel(
    near_at, far_at, near_ref, far_ref, positions_ref, momenta_ref, kick_ref, coupling_ref,
    new_positions_ref, new_momenta_ref,
):
    rows, columns = positions_ref.shape
    odd = lax.rem(lax.axis_index("rows"), 2) == 1
    lay = lambda ref, at: jnp.concatenate(
        [ref[at + g : at + g + 1, :] for g in range(columns // LANES)], axis=1
    )
    near, far = lay(near_ref, near_at), lay(far_ref, far_at)
    x = positions_ref[...]
    above = jnp.concatenate([jnp.where(odd, near, far), x[:-1]], axis=0)
    below = jnp.concatenate([x[1:], jnp.where(odd, far, near)], axis=0)
    spring = jnp.sin(above - x) + jnp.sin(below - x)
    spring = spring + jnp.sin(lane_roll(x, 1) - x)
    spring = spring + jnp.sin(lane_roll(x, -1) - x)
    momenta = momenta_ref[...] + kick_ref[...] * jnp.sin(x) + coupling_ref[...] * spring
    new_momenta_ref[...] = momenta
    new_positions_ref[...] = x + momenta


def three(value):
    first = value.astype(jnp.bfloat16).astype(jnp.float32)
    rest = value - first
    second = rest.astype(jnp.bfloat16).astype(jnp.float32)
    return first, second, (rest - second).astype(jnp.bfloat16).astype(jnp.float32)


def inverse_factor(gram, scale, weights_ref):
    order = gram.shape[0]
    step = 8
    lane = lax.broadcasted_iota(jnp.int32, (step, order), 1)
    sub = lax.broadcasted_iota(jnp.int32, (step, order), 0)
    spread = lambda value: jnp.broadcast_to(value, (step, order))
    work = [gram[at : at + step, :] for at in range(0, order, step)]
    squares = jnp.ones((step, order), jnp.float32)
    inverse = []
    for block in range(order // step):
        first = block * step
        own = work[block]
        if block == 0:
            columns = [spread(own[:, first + a : first + a + 1]) for a in range(step)]
        pivot = [
            [spread(columns[a][i : i + 1, :]) if i >= a else None for a in range(step)]
            for i in range(step)
        ]
        inside = (lane >= first) & (lane < first + step)
        extended = jnp.where(inside, jnp.where(lane - first == sub, 1.0, 0.0), own)
        solved = [spread(extended[a : a + 1, :]) for a in range(step)]
        recip = [None] * step
        lower = [[None] * step for _ in range(step)]
        ahead = None
        if block + 1 < order // step:
            ahead = work[block + 1]
            ahead_columns = [spread(ahead[:, first + a : first + a + 1]) for a in range(step)]
            coming = [
                spread(ahead[:, first + step + b : first + step + b + 1]) for b in range(step)
            ]
            ahead = jnp.where(inside, 0.0, ahead)
        for a in range(step):
            recip[a] = 1.0 / pivot[a][a]
            for i in range(a + 1, step):
                lower[i][a] = pivot[i][a] * recip[a]
            for b in range(a + 1, step):
                for i in range(b, step):
                    pivot[i][b] = pivot[i][b] - lower[i][a] * pivot[b][a]
            for i in range(a + 1, step):
                solved[i] = solved[i] - lower[i][a] * solved[a]
            if ahead is not None:
                factor = ahead_columns[a] * recip[a]
                ahead = ahead - factor * solved[a]
                for b in range(step):
                    coming[b] = coming[b] - factor * spread(ahead_columns[a][b : b + 1, :])
                for b in range(a + 1, step):
                    ahead_columns[b] = ahead_columns[b] - factor * pivot[b][a]
        if ahead is not None:
            work[block + 1], columns = ahead, coming
        scaled = [solved[a] * recip[a] for a in range(step)]
        for a in range(step - 1, 0, -1):
            for i in range(a):
                scaled[i] = scaled[i] - lower[a][i] * scaled[a]
        reach = min(block + 3, order // step)
        for later in range(block + 2, reach):
            rest = work[later]
            t = [spread(rest[:, first + a : first + a + 1]) * scaled[a] for a in range(step)]
            while len(t) > 1:
                t = [t[i] + t[i + 1] for i in range(0, len(t), 2)]
            work[later] = jnp.where(inside, 0.0, rest) - t[0]
        if reach < order // step:
            rows_y, rows_s = solved[0], solved[0] * recip[0]
            for a in range(1, step):
                rows_y = jnp.where(sub == a, solved[a], rows_y)
                rows_s = jnp.where(sub == a, solved[a] * recip[a], rows_s)
            y1, y2, y3 = three(rows_y)
            s1, s2, s3 = three(rows_s)
            left = jnp.concatenate([y1, y1, y2, y1, y3, y2], axis=0).astype(jnp.bfloat16)
            right = jnp.concatenate([s1, s2, s1, s3, s1, s2], axis=0).astype(jnp.bfloat16)
            update = lax.dot_general(
                left, right, (((0,), (0,)), ((), ())), preferred_element_type=jnp.float32
            )
            for later in range(reach, order // step):
                work[later] = jnp.where(inside, 0.0, work[later]) - update[
                    later * step : (later + 1) * step, :
                ]
        rows_out, diagonal = solved[0], pivot[0][0]
        for a in range(step):
            rows_out = jnp.where(sub == a, solved[a], rows_out)
            diagonal = jnp.where(sub == a, pivot[a][a], diagonal)
            squares = jnp.where(lane == first + a, pivot[a][a], squares)
        inverse.append(jnp.where(
            lane <= first + sub, rows_out * (scale * lax.rsqrt(diagonal)), 0.0
        ))
        if block % 2:
            factor = split_pair(jnp.concatenate(inverse[-2:], axis=0))
            high, low = factor[:, :order], factor[:, order:]
            at = first - step
            weights_ref[at : at + 2 * step, :] = jnp.concatenate([high, high], axis=1)
            weights_ref[order + at : order + at + 2 * step, :] = jnp.concatenate([low, low], axis=1)
    return squares


def ortho_kernel(
    sites_total, gram_ref, other_ref, log_growth_ref, inner_ref, near_ref, far_ref, tail_ref,
    out_ref, growth_ref,
    weights_ref, out_buf, out_sems,
):
    rows, columns = out_ref.shape[1], out_ref.shape[2]
    head = far_ref.shape[1]
    squares = inverse_factor(gram_ref[...] + other_ref[...], math.sqrt(sites_total), weights_ref)
    growth_ref[...] = (
        log_growth_ref[...] + 0.5 * jnp.log(squares[:1]) - 0.5 * math.log(sites_total)
    )
    weights = weights_ref[...]

    def product(pairs):
        both = lax.dot_general(
            pairs, weights, (((1,), (1,)), ((), ())), preferred_element_type=jnp.float32
        )
        return both[:, :LANES] + both[:, LANES:]

    stores = []
    piece = columns - head

    def send(part, slot, row):
        store = pltpu.make_async_copy(
            out_buf.at[part, slot], out_ref.at[part, row], out_sems.at[part, slot]
        )
        store.start()
        stores.append(store)

    for part in range(2):
        for r in range(rows - 2):
            for at in range(0, columns, piece):
                out_buf[part, r, at : at + piece] = product(inner_ref[part, r, at : at + piece])
            send(part, r, r + 1)
        for at in range(0, columns, piece):
            out_buf[part, rows - 2, at : at + piece] = product(near_ref[part, at : at + piece])
        send(part, rows - 2, side_slot(0) * (rows - 1))
        for at in range(0, head, piece):
            out_buf[part, rows - 1, at : at + piece] = product(far_ref[part, at : at + piece])
        out_buf[part, rows - 1, head:] = product(tail_ref[part])
        send(part, rows - 1, side_slot(1) * (rows - 1))
    for store in stores:
        store.wait()


def sum_over_rows(value, summed):
    devices = lax.axis_size("rows")
    if devices & (devices - 1):
        return lax.psum(value, "rows"), jnp.zeros_like(value)
    bit, other = 1, None
    while bit < devices:
        if other is not None:
            value = summed(value, other)
        other = lax.ppermute(value, "rows", [(i, i ^ bit) for i in range(devices)])
        bit *= 2
    return value, other


def local(positions, momenta, kick_strength, coupling, tangent, log_growth):
    rows, columns = positions.shape
    vectors = tangent.shape[3]
    devices = lax.axis_size("rows")
    groups = columns // LANES
    in_hbm = pl.BlockSpec(memory_space=pltpu.HBM)
    resident = pl.BlockSpec(memory_space=pltpu.VMEM)
    f32 = lambda *shape: pltpu.VMEM(shape, jnp.float32)
    bf16 = lambda *shape: pltpu.VMEM(shape, jnp.bfloat16)
    near_core = lambda array: pltpu.with_memory_space_constraint(array, pltpu.VMEM)
    tangent = pltpu.with_memory_space_constraint(tangent, pltpu.HBM)

    tail_sites = columns // 4 if columns % (4 * LANES) == 0 else LANES
    head = columns - tail_sites
    near, far, tail = pl.pallas_call(
        edges_kernel,
        out_shape=[
            f32(columns + groups, vectors), f32(head + groups, vectors), f32(tail_sites, vectors)
        ],
        in_specs=[in_hbm, in_hbm],
        out_specs=[resident] * 3,
        scratch_shapes=[
            pltpu.VMEM((rows, columns), jnp.float32), pltpu.SemaphoreType.DMA((4,))
        ],
        compiler_params=pltpu.CompilerParams(vmem_limit_bytes=4 * MIB),
        name="edges",
    )(tangent, pltpu.with_memory_space_constraint(positions, pltpu.HBM))
    outward = [(i, (i + 1 if i % 2 else i - 1) % devices) for i in range(devices)]
    far = lax.ppermute(far, "rows", outward)
    near = lax.ppermute(near, "rows", [(i, i ^ 1) for i in range(devices)])
    tail = lax.ppermute(tail, "rows", outward)

    inner_pairs, partial, inner_gram = pl.pallas_call(
        inner_kernel,
        out_shape=[
            bf16(2, rows - 2, columns, 2 * vectors),
            f32(2, 2, columns, vectors),
            f32(vectors, vectors),
        ],
        in_specs=[in_hbm, resident, resident, resident],
        out_specs=[resident] * 3,
        scratch_shapes=[
            pltpu.VMEM((rows, columns + 16, vectors), jnp.float32),
            pltpu.VMEM((rows, columns, vectors), jnp.float32),
            pltpu.VMEM((rows, LANES, LANES), jnp.float32),
            pltpu.SemaphoreType.DMA((2, rows)),
        ],
        compiler_params=pltpu.CompilerParams(vmem_limit_bytes=16 * MIB),
        cost_estimate=pl.CostEstimate(
            flops=2 * 10**9, bytes_accessed=8 * MIB, transcendentals=0
        ),
        name="inner",
    )(tangent, positions, kick_strength, coupling)

    def finish(name, side, first, sites, angles_at, angles, halo, before):
        return pl.pallas_call(
            functools.partial(row_gram_kernel, side, first, angles_at),
            out_shape=[bf16(2, sites, 2 * vectors), f32(vectors, vectors)],
            in_specs=[resident] * 6,
            out_specs=[resident] * 2,
            scratch_shapes=[pltpu.VMEM((LANES, LANES), jnp.float32)],
            compiler_params=pltpu.CompilerParams(vmem_limit_bytes=8 * MIB),
            cost_estimate=pl.CostEstimate(
                flops=4 * 10**8, bytes_accessed=2 * MIB, transcendentals=0
            ),
            name=name,
        )(
            near_core(angles), near_core(halo), near_core(partial), near_core(positions),
            near_core(coupling), near_core(before),
        )

    near_pairs, gram = finish("near", 0, 0, columns, columns, near, near, inner_gram)
    far_pairs, gram = finish("far", 1, 0, head, head, far, far, gram)
    tail_pairs, gram = finish("tail", 1, head, tail_sites, head, far, tail, gram)

    def summed(left, right):
        return pl.pallas_call(
            add_kernel,
            out_shape=f32(vectors, vectors),
            in_specs=[resident] * 2,
            out_specs=resident,
            compiler_params=pltpu.CompilerParams(vmem_limit_bytes=1 * MIB),
            name="gram_sum",
        )(near_core(left), near_core(right))

    gram, gram_other = sum_over_rows(gram, summed)

    new_positions, new_momenta = pl.pallas_call(
        functools.partial(angles_kernel, columns, head),
        out_shape=[jax.ShapeDtypeStruct((rows, columns), jnp.float32)] * 2,
        in_specs=[resident] * 6,
        out_specs=[resident] * 2,
        compiler_params=pltpu.CompilerParams(vmem_limit_bytes=4 * MIB),
        cost_estimate=pl.CostEstimate(flops=10**6, bytes_accessed=10**6, transcendentals=0),
        name="angles",
    )(near_core(near), near_core(far), positions, momenta, kick_strength, coupling)

    sites_total = rows * devices * columns
    tangent_out, growth = pl.pallas_call(
        functools.partial(ortho_kernel, sites_total),
        out_shape=[
            pltpu.HBM((2, rows, columns, vectors), jnp.float32),
            jax.ShapeDtypeStruct((1, vectors), jnp.float32),
        ],
        in_specs=[resident] * 7,
        out_specs=[in_hbm, resident],
        scratch_shapes=[
            pltpu.VMEM((2 * vectors, 2 * vectors), jnp.bfloat16),
            pltpu.VMEM((2, rows, columns, vectors), jnp.float32),
            pltpu.SemaphoreType.DMA((2, rows)),
        ],
        compiler_params=pltpu.CompilerParams(vmem_limit_bytes=16 * MIB),
        name="ortho",
    )(
        near_core(gram), near_core(gram_other), log_growth.reshape(1, vectors),
        near_core(inner_pairs), near_core(near_pairs), near_core(far_pairs), near_core(tail_pairs),
    )
    return (new_positions, new_momenta, tangent_out, growth.reshape(vectors))


def solution(mesh):
    placed = (
        P("rows", "groups"),
        P("rows", "groups"),
        P("rows", None),
        P("rows", None),
        P("groups", "rows", None, None),
        P("groups"),
    )
    return jax.shard_map(
        local,
        mesh=mesh,
        in_specs=placed,
        out_specs=(
            P("rows", "groups"),
            P("rows", "groups"),
            P("groups", "rows", None, None),
            P("groups"),
        ),
        check_vma=False,
    )
```

```python
import functools
import math

import jax
import jax.numpy as jnp
from jax import lax
from jax.experimental import pallas as pl
from jax.experimental.pallas import tpu as pltpu
from jax.sharding import PartitionSpec as P

LANES = 128
MIB = 1 << 20


def lane_roll(field, shift):
    return pltpu.roll(field, shift % field.shape[1], axis=1)


def split_pair(value):
    high = value.astype(jnp.bfloat16)
    low = (value - high.astype(jnp.float32)).astype(jnp.bfloat16)
    return jnp.concatenate([high, low], axis=1)


def pair_gram(pairs):
    return lax.dot_general(
        pairs, pairs, (((0,), (0,)), ((), ())), preferred_element_type=jnp.float32
    )


def fold_pairs(gram):
    half = gram.shape[0] // 2
    return (gram[:half, :half] + gram[half:, half:]) + (gram[:half, half:] + gram[half:, :half])


def edges_kernel(
    tangent_ref, positions_hbm, near_ref, far_ref, tail_ref, positions_ref, sems
):
    rows, columns = positions_ref.shape
    head = columns - tail_ref.shape[0]
    odd = lax.rem(lax.axis_index("rows"), 2)
    near_row = (1 - odd) * (rows - 1)
    far_row = rows - 1 - near_row
    near, far = tangent_ref.at[0, near_row], tangent_ref.at[0, far_row]
    copies = [
        pltpu.make_async_copy(far.at[pl.ds(0, head)], far_ref.at[pl.ds(0, head)], sems.at[0]),
        pltpu.make_async_copy(far.at[pl.ds(head, columns - head)], tail_ref, sems.at[1]),
        pltpu.make_async_copy(near, near_ref.at[pl.ds(0, columns)], sems.at[2]),
    ]
    angle_copy = pltpu.make_async_copy(positions_hbm, positions_ref, sems.at[3])
    angle_copy.start()
    for copy in copies:
        copy.start()
    angle_copy.wait()
    for row, at, out in ((near_row, columns, near_ref), (far_row, head, far_ref)):
        angles = positions_ref[pl.ds(row, 1), :]
        for group in range(columns // LANES):
            out[at + group : at + group + 1, :] = angles[:, group * LANES : (group + 1) * LANES]
    for copy in copies:
        copy.wait()


def inner_kernel(
    tangent_ref, positions_ref, kick_ref, coupling_ref,
    pairs_ref, partial_ref, gram_ref,
    pos_pad, mom_buf, stack, sems,
):
    rows, columns = positions_ref.shape
    groups = columns // LANES
    order = [*range(rows)]
    pos_copies = [
        pltpu.make_async_copy(
            tangent_ref.at[0, r], pos_pad.at[r, pl.ds(8, columns)], sems.at[0, r]
        )
        for r in order
    ]
    mom_copies = [
        pltpu.make_async_copy(tangent_ref.at[1, r], mom_buf.at[r], sems.at[1, r]) for r in order
    ]
    for r in order:
        pos_copies[r].start()
        mom_copies[r].start()

    x = positions_ref[...]
    coupling = coupling_ref[...]
    left = coupling * jnp.cos(lane_roll(x, 1) - x)
    right = coupling * jnp.cos(lane_roll(x, -1) - x)
    vertical = jnp.cos(x[1:] - x[:-1])
    none = jnp.zeros((1, columns), jnp.float32)
    up = coupling * jnp.concatenate([none, vertical], axis=0)
    down = coupling * jnp.concatenate([vertical, none], axis=0)
    centre = kick_ref[...] * jnp.cos(x) - ((left + right) + (up + down))
    for k, weight in enumerate((centre, left, right, up, down)):
        for r in range(rows):
            for group in range(groups):
                at = k * groups + group
                stack[r, at : at + 1, :] = weight[r : r + 1, group * LANES : (group + 1) * LANES]

    for r in order:
        pos_copies[r].wait()
        mom_copies[r].wait()
        pos_pad[r, 7:8, :] = pos_pad[r, 7 + columns : 8 + columns, :]
        pos_pad[r, 8 + columns : 9 + columns, :] = pos_pad[r, 8:9, :]

    def stepped(r, group, table, sides):
        at = 8 + group * LANES
        factor = lambda k: jnp.broadcast_to(
            table[:, k * groups + group : k * groups + group + 1], (LANES, LANES)
        )
        u = pos_pad[r, at : at + LANES, :]
        total = mom_buf[r, group * LANES : (group + 1) * LANES, :] + factor(0) * u
        total = total + factor(1) * pos_pad[r, at - 1 : at - 1 + LANES, :]
        total = total + factor(2) * pos_pad[r, at + 1 : at + 1 + LANES, :]
        for k, other in sides:
            total = total + factor(k) * pos_pad[other, at : at + LANES, :]
        return u, total

    for slot, (r, sides) in enumerate(((0, ((4, 1),)), (rows - 1, ((3, rows - 2),)))):
        table = stack[r].T
        for group in range(groups):
            u, total = stepped(r, group, table, sides)
            partial_ref[0, slot, group * LANES : (group + 1) * LANES, :] = u
            partial_ref[1, slot, group * LANES : (group + 1) * LANES, :] = total

    gram = jnp.zeros((2 * LANES, 2 * LANES), jnp.float32)
    for r in range(1, rows - 1):
        table = stack[r].T
        for group in range(groups):
            u, mom = stepped(r, group, table, ((3, r - 1), (4, r + 1)))
            span = pl.ds(group * LANES, LANES)
            pairs_ref[0, r - 1, span, :] = split_pair(u + mom)
            pairs_ref[1, r - 1, span, :] = split_pair(mom)
        for part in range(2):
            gram = gram + pair_gram(pairs_ref[part, r - 1])
    gram_ref[...] = fold_pairs(gram)


def side_slot(side):
    odd = lax.rem(lax.axis_index("rows"), 2)
    return odd if side else 1 - odd


def row_gram_kernel(
    side, first, angles_at, angles_ref, halo_ref, partial_ref, positions_ref, coupling_ref,
    before_ref, pairs_ref, gram_ref, stack,
):
    columns = positions_ref.shape[1]
    sites = pairs_ref.shape[1]
    slot = side_slot(side)
    row = slot * (positions_ref.shape[0] - 1)
    x = positions_ref[pl.ds(row, 1), :]
    coupling = coupling_ref[pl.ds(row, 1), :]
    for group in range(sites // LANES):
        span = slice(first + group * LANES, first + (group + 1) * LANES)
        at = angles_at + first // LANES + group
        stack[group : group + 1, :] = coupling[:, span] * jnp.cos(
            angles_ref[at : at + 1, :] - x[:, span]
        )
    table = stack[...].T
    for group in range(sites // LANES):
        span = slice(group * LANES, (group + 1) * LANES)
        from_first = slice(first + group * LANES, first + (group + 1) * LANES)
        factor = jnp.broadcast_to(table[:, group : group + 1], (LANES, LANES))
        u = partial_ref[0, slot, from_first, :]
        mom = partial_ref[1, slot, from_first, :] + factor * (halo_ref[span, :] - u)
        pairs_ref[0, span, :] = split_pair(u + mom)
        pairs_ref[1, span, :] = split_pair(mom)
    gram = pair_gram(pairs_ref[0]) + pair_gram(pairs_ref[1])
    gram_ref[...] = before_ref[...] + fold_pairs(gram)


def pairwise(terms):
    while len(terms) > 1:
        terms = [
            terms[i] + terms[i + 1] if i + 1 < len(terms) else terms[i]
            for i in range(0, len(terms), 2)
        ]
    return terms[0]


def add_kernel(*refs):
    refs[-1][...] = pairwise([ref[...] for ref in refs[:-1]])


def angles_kernel(
    near_at, far_at, near_ref, far_ref, positions_ref, momenta_ref, kick_ref, coupling_ref,
    new_positions_ref, new_momenta_ref,
):
    rows, columns = positions_ref.shape
    odd = lax.rem(lax.axis_index("rows"), 2) == 1
    lay = lambda ref, at: jnp.concatenate(
        [ref[at + g : at + g + 1, :] for g in range(columns // LANES)], axis=1
    )
    near, far = lay(near_ref, near_at), lay(far_ref, far_at)
    x = positions_ref[...]
    above = jnp.concatenate([jnp.where(odd, near, far), x[:-1]], axis=0)
    below = jnp.concatenate([x[1:], jnp.where(odd, far, near)], axis=0)
    spring = jnp.sin(above - x) + jnp.sin(below - x)
    spring = spring + jnp.sin(lane_roll(x, 1) - x)
    spring = spring + jnp.sin(lane_roll(x, -1) - x)
    momenta = momenta_ref[...] + kick_ref[...] * jnp.sin(x) + coupling_ref[...] * spring
    new_momenta_ref[...] = momenta
    new_positions_ref[...] = x + momenta


def three(value):
    first = value.astype(jnp.bfloat16).astype(jnp.float32)
    rest = value - first
    second = rest.astype(jnp.bfloat16).astype(jnp.float32)
    return first, second, (rest - second).astype(jnp.bfloat16).astype(jnp.float32)


def inverse_factor(gram, scale, weights_ref):
    order = gram.shape[0]
    step = 8
    lane = lax.broadcasted_iota(jnp.int32, (step, order), 1)
    sub = lax.broadcasted_iota(jnp.int32, (step, order), 0)
    spread = lambda value: jnp.broadcast_to(value, (step, order))
    work = [gram[at : at + step, :] for at in range(0, order, step)]
    squares = jnp.ones((step, order), jnp.float32)
    inverse = []
    for block in range(order // step):
        first = block * step
        own = work[block]
        if block == 0:
            columns = [spread(own[:, first + a : first + a + 1]) for a in range(step)]
        pivot = [
            [spread(columns[a][i : i + 1, :]) if i >= a else None for a in range(step)]
            for i in range(step)
        ]
        inside = (lane >= first) & (lane < first + step)
        extended = jnp.where(inside, jnp.where(lane - first == sub, 1.0, 0.0), own)
        solved = [spread(extended[a : a + 1, :]) for a in range(step)]
        recip = [None] * step
        lower = [[None] * step for _ in range(step)]
        ahead = None
        if block + 1 < order // step:
            ahead = work[block + 1]
            ahead_columns = [spread(ahead[:, first + a : first + a + 1]) for a in range(step)]
            coming = [
                spread(ahead[:, first + step + b : first + step + b + 1]) for b in range(step)
            ]
            ahead = jnp.where(inside, 0.0, ahead)
        for a in range(step):
            recip[a] = 1.0 / pivot[a][a]
            for i in range(a + 1, step):
                lower[i][a] = pivot[i][a] * recip[a]
            for b in range(a + 1, step):
                for i in range(b, step):
                    pivot[i][b] = pivot[i][b] - lower[i][a] * pivot[b][a]
            for i in range(a + 1, step):
                solved[i] = solved[i] - lower[i][a] * solved[a]
            if ahead is not None:
                factor = ahead_columns[a] * recip[a]
                ahead = ahead - factor * solved[a]
                for b in range(step):
                    coming[b] = coming[b] - factor * spread(ahead_columns[a][b : b + 1, :])
                for b in range(a + 1, step):
                    ahead_columns[b] = ahead_columns[b] - factor * pivot[b][a]
        if ahead is not None:
            work[block + 1], columns = ahead, coming
        scaled = [solved[a] * recip[a] for a in range(step)]
        for a in range(step - 1, 0, -1):
            for i in range(a):
                scaled[i] = scaled[i] - lower[a][i] * scaled[a]
        reach = min(block + 3, order // step)
        for later in range(block + 2, reach):
            rest = work[later]
            t = [spread(rest[:, first + a : first + a + 1]) * scaled[a] for a in range(step)]
            while len(t) > 1:
                t = [t[i] + t[i + 1] for i in range(0, len(t), 2)]
            work[later] = jnp.where(inside, 0.0, rest) - t[0]
        if reach < order // step:
            rows_y, rows_s = solved[0], solved[0] * recip[0]
            for a in range(1, step):
                rows_y = jnp.where(sub == a, solved[a], rows_y)
                rows_s = jnp.where(sub == a, solved[a] * recip[a], rows_s)
            y1, y2, y3 = three(rows_y)
            s1, s2, s3 = three(rows_s)
            left = jnp.concatenate([y1, y1, y2, y1, y3, y2], axis=0).astype(jnp.bfloat16)
            right = jnp.concatenate([s1, s2, s1, s3, s1, s2], axis=0).astype(jnp.bfloat16)
            update = lax.dot_general(
                left, right, (((0,), (0,)), ((), ())), preferred_element_type=jnp.float32
            )
            for later in range(reach, order // step):
                work[later] = jnp.where(inside, 0.0, work[later]) - update[
                    later * step : (later + 1) * step, :
                ]
        rows_out, diagonal = solved[0], pivot[0][0]
        for a in range(step):
            rows_out = jnp.where(sub == a, solved[a], rows_out)
            diagonal = jnp.where(sub == a, pivot[a][a], diagonal)
            squares = jnp.where(lane == first + a, pivot[a][a], squares)
        inverse.append(jnp.where(
            lane <= first + sub, rows_out * (scale * lax.rsqrt(diagonal)), 0.0
        ))
        if block % 2:
            factor = split_pair(jnp.concatenate(inverse[-2:], axis=0))
            high, low = factor[:, :order], factor[:, order:]
            at = first - step
            weights_ref[at : at + 2 * step, :] = jnp.concatenate([high, high], axis=1)
            weights_ref[order + at : order + at + 2 * step, :] = jnp.concatenate([low, low], axis=1)
    return squares


def ortho_kernel(
    sites_total, gram_ref, other_ref, log_growth_ref, inner_ref, near_ref, far_ref, tail_ref,
    out_ref, growth_ref,
    weights_ref, out_buf, out_sems,
):
    rows, columns = out_ref.shape[1], out_ref.shape[2]
    head = far_ref.shape[1]
    squares = inverse_factor(gram_ref[...] + other_ref[...], math.sqrt(sites_total), weights_ref)
    growth_ref[...] = (
        log_growth_ref[...] + 0.5 * jnp.log(squares[:1]) - 0.5 * math.log(sites_total)
    )
    weights = weights_ref[...]

    def product(pairs):
        both = lax.dot_general(
            pairs, weights, (((1,), (1,)), ((), ())), preferred_element_type=jnp.float32
        )
        return both[:, :LANES] + both[:, LANES:]

    stores = []
    piece = columns - head

    def send(part, slot, row):
        store = pltpu.make_async_copy(
            out_buf.at[part, slot], out_ref.at[part, row], out_sems.at[part, slot]
        )
        store.start()
        stores.append(store)

    for part in range(2):
        for r in range(rows - 2):
            for at in range(0, columns, piece):
                out_buf[part, r, at : at + piece] = product(inner_ref[part, r, at : at + piece])
            send(part, r, r + 1)
        for at in range(0, columns, piece):
            out_buf[part, rows - 2, at : at + piece] = product(near_ref[part, at : at + piece])
        send(part, rows - 2, side_slot(0) * (rows - 1))
        for at in range(0, head, piece):
            out_buf[part, rows - 1, at : at + piece] = product(far_ref[part, at : at + piece])
        out_buf[part, rows - 1, head:] = product(tail_ref[part])
        send(part, rows - 1, side_slot(1) * (rows - 1))
    for store in stores:
        store.wait()


def sum_over_rows(value, summed):
    devices = lax.axis_size("rows")
    if devices & (devices - 1):
        return [lax.psum(value, "rows"), jnp.zeros_like(value)]
    bits = [1 << k for k in range(devices.bit_length() - 1)]
    stages = [bits[:1]]
    if len(bits) > 2:
        stages.append([bits[1], bits[2], bits[1] + bits[2]])
        bits = bits[3:]
    else:
        bits = bits[1:]
    stages.extend([bit] for bit in bits)
    terms = [value]
    for stage in stages:
        if len(terms) > 1:
            terms = [summed(terms)]
        terms.extend([
            lax.ppermute(terms[0], "rows", [(i, i ^ offset) for i in range(devices)])
            for offset in stage
        ])
    return terms


def local(positions, momenta, kick_strength, coupling, tangent, log_growth):
    rows, columns = positions.shape
    vectors = tangent.shape[3]
    devices = lax.axis_size("rows")
    groups = columns // LANES
    in_hbm = pl.BlockSpec(memory_space=pltpu.HBM)
    resident = pl.BlockSpec(memory_space=pltpu.VMEM)
    f32 = lambda *shape: pltpu.VMEM(shape, jnp.float32)
    bf16 = lambda *shape: pltpu.VMEM(shape, jnp.bfloat16)
    near_core = lambda array: pltpu.with_memory_space_constraint(array, pltpu.VMEM)
    tangent = pltpu.with_memory_space_constraint(tangent, pltpu.HBM)

    tail_sites = columns // 4 if columns % (4 * LANES) == 0 else LANES
    head = columns - tail_sites
    near, far, tail = pl.pallas_call(
        edges_kernel,
        out_shape=[
            f32(columns + groups, vectors), f32(head + groups, vectors), f32(tail_sites, vectors)
        ],
        in_specs=[in_hbm, in_hbm],
        out_specs=[resident] * 3,
        scratch_shapes=[
            pltpu.VMEM((rows, columns), jnp.float32), pltpu.SemaphoreType.DMA((4,))
        ],
        compiler_params=pltpu.CompilerParams(vmem_limit_bytes=4 * MIB),
        name="edges",
    )(tangent, pltpu.with_memory_space_constraint(positions, pltpu.HBM))
    outward = [(i, (i + 1 if i % 2 else i - 1) % devices) for i in range(devices)]
    far = lax.ppermute(far, "rows", outward)
    near = lax.ppermute(near, "rows", [(i, i ^ 1) for i in range(devices)])
    tail = lax.ppermute(tail, "rows", outward)

    inner_pairs, partial, inner_gram = pl.pallas_call(
        inner_kernel,
        out_shape=[
            bf16(2, rows - 2, columns, 2 * vectors),
            f32(2, 2, columns, vectors),
            f32(vectors, vectors),
        ],
        in_specs=[in_hbm, resident, resident, resident],
        out_specs=[resident] * 3,
        scratch_shapes=[
            pltpu.VMEM((rows, columns + 16, vectors), jnp.float32),
            pltpu.VMEM((rows, columns, vectors), jnp.float32),
            pltpu.VMEM((rows, LANES, LANES), jnp.float32),
            pltpu.SemaphoreType.DMA((2, rows)),
        ],
        compiler_params=pltpu.CompilerParams(vmem_limit_bytes=16 * MIB),
        cost_estimate=pl.CostEstimate(
            flops=2 * 10**9, bytes_accessed=8 * MIB, transcendentals=0
        ),
        name="inner",
    )(tangent, positions, kick_strength, coupling)

    def finish(name, side, first, sites, angles_at, angles, halo, before):
        return pl.pallas_call(
            functools.partial(row_gram_kernel, side, first, angles_at),
            out_shape=[bf16(2, sites, 2 * vectors), f32(vectors, vectors)],
            in_specs=[resident] * 6,
            out_specs=[resident] * 2,
            scratch_shapes=[pltpu.VMEM((LANES, LANES), jnp.float32)],
            compiler_params=pltpu.CompilerParams(vmem_limit_bytes=8 * MIB),
            cost_estimate=pl.CostEstimate(
                flops=4 * 10**8, bytes_accessed=2 * MIB, transcendentals=0
            ),
            name=name,
        )(
            near_core(angles), near_core(halo), near_core(partial), near_core(positions),
            near_core(coupling), near_core(before),
        )

    near_pairs, gram = finish("near", 0, 0, columns, columns, near, near, inner_gram)
    far_pairs, gram = finish("far", 1, 0, head, head, far, far, gram)
    tail_pairs, gram = finish("tail", 1, head, tail_sites, head, far, tail, gram)

    def summed(terms):
        return pl.pallas_call(
            add_kernel,
            out_shape=f32(vectors, vectors),
            in_specs=[resident] * len(terms),
            out_specs=resident,
            compiler_params=pltpu.CompilerParams(vmem_limit_bytes=1 * MIB),
            name="gram_sum",
        )(*[near_core(term) for term in terms])

    terms = sum_over_rows(gram, summed)
    if len(terms) > 2:
        terms = [summed(terms), jnp.zeros_like(gram)]
    gram, gram_other = terms

    new_positions, new_momenta = pl.pallas_call(
        functools.partial(angles_kernel, columns, head),
        out_shape=[jax.ShapeDtypeStruct((rows, columns), jnp.float32)] * 2,
        in_specs=[resident] * 6,
        out_specs=[resident] * 2,
        compiler_params=pltpu.CompilerParams(vmem_limit_bytes=4 * MIB),
        cost_estimate=pl.CostEstimate(flops=10**6, bytes_accessed=10**6, transcendentals=0),
        name="angles",
    )(near_core(near), near_core(far), positions, momenta, kick_strength, coupling)

    sites_total = rows * devices * columns
    tangent_out, growth = pl.pallas_call(
        functools.partial(ortho_kernel, sites_total),
        out_shape=[
            pltpu.HBM((2, rows, columns, vectors), jnp.float32),
            jax.ShapeDtypeStruct((1, vectors), jnp.float32),
        ],
        in_specs=[resident] * 7,
        out_specs=[in_hbm, resident],
        scratch_shapes=[
            pltpu.VMEM((2 * vectors, 2 * vectors), jnp.bfloat16),
            pltpu.VMEM((2, rows, columns, vectors), jnp.float32),
            pltpu.SemaphoreType.DMA((2, rows)),
        ],
        compiler_params=pltpu.CompilerParams(vmem_limit_bytes=16 * MIB),
        name="ortho",
    )(
        near_core(gram), near_core(gram_other), log_growth.reshape(1, vectors),
        near_core(inner_pairs), near_core(near_pairs), near_core(far_pairs), near_core(tail_pairs),
    )
    return (new_positions, new_momenta, tangent_out, growth.reshape(vectors))


def solution(mesh):
    placed = (
        P("rows", "groups"),
        P("rows", "groups"),
        P("rows", None),
        P("rows", None),
        P("groups", "rows", None, None),
        P("groups"),
    )
    return jax.shard_map(
        local,
        mesh=mesh,
        in_specs=placed,
        out_specs=(
            P("rows", "groups"),
            P("rows", "groups"),
            P("groups", "rows", None, None),
            P("groups"),
        ),
        check_vma=False,
    )
```

```python
import functools
import math

import jax
import jax.numpy as jnp
from jax import lax
from jax.experimental import pallas as pl
from jax.experimental.pallas import tpu as pltpu
from jax.sharding import PartitionSpec as P

LANES = 128
MIB = 1 << 20


def lane_roll(field, shift):
    return pltpu.roll(field, shift % field.shape[1], axis=1)


def split_pair(value):
    high = value.astype(jnp.bfloat16)
    low = (value - high.astype(jnp.float32)).astype(jnp.bfloat16)
    return jnp.concatenate([high, low], axis=1)


def pair_gram(pairs):
    return lax.dot_general(
        pairs, pairs, (((0,), (0,)), ((), ())), preferred_element_type=jnp.float32
    )


def fold_pairs(gram):
    half = gram.shape[0] // 2
    return (gram[:half, :half] + gram[half:, half:]) + (gram[:half, half:] + gram[half:, :half])


def edges_kernel(
    tangent_ref, positions_hbm, near_ref, far_ref, tail_ref, positions_ref, sems
):
    rows, columns = positions_ref.shape
    head = columns - tail_ref.shape[0]
    odd = lax.rem(lax.axis_index("rows"), 2)
    near_row = (1 - odd) * (rows - 1)
    far_row = rows - 1 - near_row
    near, far = tangent_ref.at[0, near_row], tangent_ref.at[0, far_row]
    copies = [
        pltpu.make_async_copy(far.at[pl.ds(0, head)], far_ref.at[pl.ds(0, head)], sems.at[0]),
        pltpu.make_async_copy(far.at[pl.ds(head, columns - head)], tail_ref, sems.at[1]),
        pltpu.make_async_copy(near, near_ref.at[pl.ds(0, columns)], sems.at[2]),
    ]
    angle_copy = pltpu.make_async_copy(positions_hbm, positions_ref, sems.at[3])
    angle_copy.start()
    for copy in copies:
        copy.start()
    angle_copy.wait()
    for row, at, out in ((near_row, columns, near_ref), (far_row, head, far_ref)):
        angles = positions_ref[pl.ds(row, 1), :]
        for group in range(columns // LANES):
            out[at + group : at + group + 1, :] = angles[:, group * LANES : (group + 1) * LANES]
    for copy in copies:
        copy.wait()


def inner_kernel(
    tangent_ref, positions_ref, kick_ref, coupling_ref,
    pairs_ref, partial_ref, gram_ref,
    pos_pad, mom_buf, stack, sems,
):
    rows, columns = positions_ref.shape
    groups = columns // LANES
    order = [*range(rows)]
    pos_copies = [
        pltpu.make_async_copy(
            tangent_ref.at[0, r], pos_pad.at[r, pl.ds(8, columns)], sems.at[0, r]
        )
        for r in order
    ]
    mom_copies = [
        pltpu.make_async_copy(tangent_ref.at[1, r], mom_buf.at[r], sems.at[1, r]) for r in order
    ]
    for r in order:
        pos_copies[r].start()
        mom_copies[r].start()

    x = positions_ref[...]
    coupling = coupling_ref[...]
    left = coupling * jnp.cos(lane_roll(x, 1) - x)
    right = coupling * jnp.cos(lane_roll(x, -1) - x)
    vertical = jnp.cos(x[1:] - x[:-1])
    none = jnp.zeros((1, columns), jnp.float32)
    up = coupling * jnp.concatenate([none, vertical], axis=0)
    down = coupling * jnp.concatenate([vertical, none], axis=0)
    centre = kick_ref[...] * jnp.cos(x) - ((left + right) + (up + down))
    for k, weight in enumerate((centre, left, right, up, down)):
        for r in range(rows):
            for group in range(groups):
                at = k * groups + group
                stack[r, at : at + 1, :] = weight[r : r + 1, group * LANES : (group + 1) * LANES]

    for r in order:
        pos_copies[r].wait()
        mom_copies[r].wait()
        pos_pad[r, 7:8, :] = pos_pad[r, 7 + columns : 8 + columns, :]
        pos_pad[r, 8 + columns : 9 + columns, :] = pos_pad[r, 8:9, :]

    def stepped(r, group, table, sides):
        at = 8 + group * LANES
        factor = lambda k: jnp.broadcast_to(
            table[:, k * groups + group : k * groups + group + 1], (LANES, LANES)
        )
        u = pos_pad[r, at : at + LANES, :]
        total = mom_buf[r, group * LANES : (group + 1) * LANES, :] + factor(0) * u
        total = total + factor(1) * pos_pad[r, at - 1 : at - 1 + LANES, :]
        total = total + factor(2) * pos_pad[r, at + 1 : at + 1 + LANES, :]
        for k, other in sides:
            total = total + factor(k) * pos_pad[other, at : at + LANES, :]
        return u, total

    for slot, (r, sides) in enumerate(((0, ((4, 1),)), (rows - 1, ((3, rows - 2),)))):
        table = stack[r].T
        for group in range(groups):
            u, total = stepped(r, group, table, sides)
            partial_ref[0, slot, group * LANES : (group + 1) * LANES, :] = u
            partial_ref[1, slot, group * LANES : (group + 1) * LANES, :] = total

    gram = jnp.zeros((2 * LANES, 2 * LANES), jnp.float32)
    for r in range(1, rows - 1):
        table = stack[r].T
        for group in range(groups):
            u, mom = stepped(r, group, table, ((3, r - 1), (4, r + 1)))
            span = pl.ds(group * LANES, LANES)
            pairs_ref[0, r - 1, span, :] = split_pair(u + mom)
            pairs_ref[1, r - 1, span, :] = split_pair(mom)
        for part in range(2):
            gram = gram + pair_gram(pairs_ref[part, r - 1])
    gram_ref[...] = fold_pairs(gram)


def side_slot(side):
    odd = lax.rem(lax.axis_index("rows"), 2)
    return odd if side else 1 - odd


def pack_symmetric(gram):
    half = gram.shape[0] // 2
    shape = (half, 2 * half)
    row = lax.broadcasted_iota(jnp.int32, shape, 0)
    lane = lax.broadcasted_iota(jnp.int32, shape, 1)
    corner = lane_roll(gram[half:], half)
    top = jnp.where((lane < half) & (lane > row), corner, gram[:half])
    diagonal = jnp.sum(jnp.where(lane == row, corner, 0.0), axis=0, keepdims=True)
    return jnp.concatenate([top, jnp.broadcast_to(diagonal, (8, 2 * half))], axis=0)


def unpack_symmetric(packed):
    order = packed.shape[1]
    half = order // 2
    top = packed[:half]
    row = lax.broadcasted_iota(jnp.int32, (half, order), 0)
    lane = lax.broadcasted_iota(jnp.int32, (half, order), 1)
    on = lane == row
    upper = jnp.where((lane >= half) | (lane < row), top, jnp.where(on, 0.5 * top, 0.0))
    corner = jnp.where(
        (lane < half) & (lane > row), top, jnp.where(on, 0.5 * packed[half : half + 1], 0.0)
    )
    triangle = jnp.concatenate([upper, lane_roll(corner, half)], axis=0)
    return triangle + triangle.T


def finish_sites(table, first_group, first, slot, halo_ref, partial_ref, pairs_ref):
    for group in range(pairs_ref.shape[1] // LANES):
        span = slice(group * LANES, (group + 1) * LANES)
        from_first = slice(first + group * LANES, first + (group + 1) * LANES)
        at = first_group + group
        factor = jnp.broadcast_to(table[:, at : at + 1], (LANES, LANES))
        u = partial_ref[0, slot, from_first, :]
        mom = partial_ref[1, slot, from_first, :] + factor * (halo_ref[span, :] - u)
        pairs_ref[0, span, :] = split_pair(u + mom)
        pairs_ref[1, span, :] = split_pair(mom)
    return fold_pairs(pair_gram(pairs_ref[0]) + pair_gram(pairs_ref[1]))


def row_gram_kernel(
    side, halo_ref, partial_ref, positions_ref, coupling_ref, before_ref,
    pairs_ref, gram_ref, table_ref, stack,
):
    columns = positions_ref.shape[1]
    sites = pairs_ref.shape[1]
    slot = side_slot(side)
    row = slot * (positions_ref.shape[0] - 1)
    x = positions_ref[pl.ds(row, 1), :]
    coupling = coupling_ref[pl.ds(row, 1), :]
    for group in range(columns // LANES):
        span = slice(group * LANES, (group + 1) * LANES)
        stack[group : group + 1, :] = coupling[:, span] * jnp.cos(
            halo_ref[sites + group : sites + group + 1, :] - x[:, span]
        )
    table = stack[...].T
    table_ref[...] = table
    gram = finish_sites(table, 0, 0, slot, halo_ref, partial_ref, pairs_ref)
    gram_ref[...] = before_ref[...] + gram


def tail_gram_kernel(first, halo_ref, partial_ref, table_ref, before_ref, pairs_ref, packed_ref):
    gram = finish_sites(
        table_ref[...], first // LANES, first, side_slot(1), halo_ref, partial_ref, pairs_ref
    )
    packed_ref[...] = pack_symmetric(before_ref[...] + gram)


def pairwise(terms):
    while len(terms) > 1:
        terms = [
            terms[i] + terms[i + 1] if i + 1 < len(terms) else terms[i]
            for i in range(0, len(terms), 2)
        ]
    return terms[0]


def add_kernel(*refs):
    refs[-1][...] = pairwise([ref[...] for ref in refs[:-1]])


def angles_kernel(
    near_at, far_at, near_ref, far_ref, positions_ref, momenta_ref, kick_ref, coupling_ref,
    new_positions_ref, new_momenta_ref,
):
    rows, columns = positions_ref.shape
    odd = lax.rem(lax.axis_index("rows"), 2) == 1
    lay = lambda ref, at: jnp.concatenate(
        [ref[at + g : at + g + 1, :] for g in range(columns // LANES)], axis=1
    )
    near, far = lay(near_ref, near_at), lay(far_ref, far_at)
    x = positions_ref[...]
    above = jnp.concatenate([jnp.where(odd, near, far), x[:-1]], axis=0)
    below = jnp.concatenate([x[1:], jnp.where(odd, far, near)], axis=0)
    spring = jnp.sin(above - x) + jnp.sin(below - x)
    spring = spring + jnp.sin(lane_roll(x, 1) - x)
    spring = spring + jnp.sin(lane_roll(x, -1) - x)
    momenta = momenta_ref[...] + kick_ref[...] * jnp.sin(x) + coupling_ref[...] * spring
    new_momenta_ref[...] = momenta
    new_positions_ref[...] = x + momenta


def three(value):
    first = value.astype(jnp.bfloat16).astype(jnp.float32)
    rest = value - first
    second = rest.astype(jnp.bfloat16).astype(jnp.float32)
    return first, second, (rest - second).astype(jnp.bfloat16).astype(jnp.float32)


def inverse_factor(gram, scale, weights_ref):
    order = gram.shape[0]
    step = 8
    lane = lax.broadcasted_iota(jnp.int32, (step, order), 1)
    sub = lax.broadcasted_iota(jnp.int32, (step, order), 0)
    spread = lambda value: jnp.broadcast_to(value, (step, order))
    work = [gram[at : at + step, :] for at in range(0, order, step)]
    squares = jnp.ones((step, order), jnp.float32)
    inverse = []
    for block in range(order // step):
        first = block * step
        own = work[block]
        if block == 0:
            columns = [spread(own[:, first + a : first + a + 1]) for a in range(step)]
        pivot = [
            [spread(columns[a][i : i + 1, :]) if i >= a else None for a in range(step)]
            for i in range(step)
        ]
        inside = (lane >= first) & (lane < first + step)
        extended = jnp.where(inside, jnp.where(lane - first == sub, 1.0, 0.0), own)
        solved = [spread(extended[a : a + 1, :]) for a in range(step)]
        recip = [None] * step
        lower = [[None] * step for _ in range(step)]
        ahead = None
        if block + 1 < order // step:
            ahead = work[block + 1]
            ahead_columns = [spread(ahead[:, first + a : first + a + 1]) for a in range(step)]
            coming = [
                spread(ahead[:, first + step + b : first + step + b + 1]) for b in range(step)
            ]
            ahead = jnp.where(inside, 0.0, ahead)
        for a in range(step):
            recip[a] = 1.0 / pivot[a][a]
            for i in range(a + 1, step):
                lower[i][a] = pivot[i][a] * recip[a]
            for b in range(a + 1, step):
                for i in range(b, step):
                    pivot[i][b] = pivot[i][b] - lower[i][a] * pivot[b][a]
            for i in range(a + 1, step):
                solved[i] = solved[i] - lower[i][a] * solved[a]
            if ahead is not None:
                factor = ahead_columns[a] * recip[a]
                ahead = ahead - factor * solved[a]
                for b in range(step):
                    coming[b] = coming[b] - factor * spread(ahead_columns[a][b : b + 1, :])
                for b in range(a + 1, step):
                    ahead_columns[b] = ahead_columns[b] - factor * pivot[b][a]
        if ahead is not None:
            work[block + 1], columns = ahead, coming
        scaled = [solved[a] * recip[a] for a in range(step)]
        for a in range(step - 1, 0, -1):
            for i in range(a):
                scaled[i] = scaled[i] - lower[a][i] * scaled[a]
        reach = min(block + 3, order // step)
        for later in range(block + 2, reach):
            rest = work[later]
            t = [spread(rest[:, first + a : first + a + 1]) * scaled[a] for a in range(step)]
            while len(t) > 1:
                t = [t[i] + t[i + 1] for i in range(0, len(t), 2)]
            work[later] = jnp.where(inside, 0.0, rest) - t[0]
        if reach < order // step:
            rows_y, rows_s = solved[0], solved[0] * recip[0]
            for a in range(1, step):
                rows_y = jnp.where(sub == a, solved[a], rows_y)
                rows_s = jnp.where(sub == a, solved[a] * recip[a], rows_s)
            y1, y2, y3 = three(rows_y)
            s1, s2, s3 = three(rows_s)
            left = jnp.concatenate([y1, y1, y2, y1, y3, y2], axis=0).astype(jnp.bfloat16)
            right = jnp.concatenate([s1, s2, s1, s3, s1, s2], axis=0).astype(jnp.bfloat16)
            update = lax.dot_general(
                left, right, (((0,), (0,)), ((), ())), preferred_element_type=jnp.float32
            )
            for later in range(reach, order // step):
                work[later] = jnp.where(inside, 0.0, work[later]) - update[
                    later * step : (later + 1) * step, :
                ]
        rows_out, diagonal = solved[0], pivot[0][0]
        for a in range(step):
            rows_out = jnp.where(sub == a, solved[a], rows_out)
            diagonal = jnp.where(sub == a, pivot[a][a], diagonal)
            squares = jnp.where(lane == first + a, pivot[a][a], squares)
        inverse.append(jnp.where(
            lane <= first + sub, rows_out * (scale * lax.rsqrt(diagonal)), 0.0
        ))
        if block % 2:
            factor = split_pair(jnp.concatenate(inverse[-2:], axis=0))
            high, low = factor[:, :order], factor[:, order:]
            at = first - step
            weights_ref[at : at + 2 * step, :] = jnp.concatenate([high, high], axis=1)
            weights_ref[order + at : order + at + 2 * step, :] = jnp.concatenate([low, low], axis=1)
    return squares


def ortho_kernel(
    sites_total, gram_ref, other_ref, log_growth_ref, inner_ref, near_ref, far_ref, tail_ref,
    out_ref, growth_ref,
    weights_ref, out_buf, out_sems,
):
    rows, columns = out_ref.shape[1], out_ref.shape[2]
    head = far_ref.shape[1]
    squares = inverse_factor(
        unpack_symmetric(gram_ref[...] + other_ref[...]), math.sqrt(sites_total), weights_ref
    )
    growth_ref[...] = (
        log_growth_ref[...] + 0.5 * jnp.log(squares[:1]) - 0.5 * math.log(sites_total)
    )
    weights = weights_ref[...]

    def product(pairs):
        both = lax.dot_general(
            pairs, weights, (((1,), (1,)), ((), ())), preferred_element_type=jnp.float32
        )
        return both[:, :LANES] + both[:, LANES:]

    stores = []
    piece = columns - head

    def send(part, slot, row):
        store = pltpu.make_async_copy(
            out_buf.at[part, slot], out_ref.at[part, row], out_sems.at[part, slot]
        )
        store.start()
        stores.append(store)

    for part in range(2):
        for r in range(rows - 2):
            for at in range(0, columns, piece):
                out_buf[part, r, at : at + piece] = product(inner_ref[part, r, at : at + piece])
            send(part, r, r + 1)
        for at in range(0, columns, piece):
            out_buf[part, rows - 2, at : at + piece] = product(near_ref[part, at : at + piece])
        send(part, rows - 2, side_slot(0) * (rows - 1))
        for at in range(0, head, piece):
            out_buf[part, rows - 1, at : at + piece] = product(far_ref[part, at : at + piece])
        out_buf[part, rows - 1, head:] = product(tail_ref[part])
        send(part, rows - 1, side_slot(1) * (rows - 1))
    for store in stores:
        store.wait()


def sum_over_rows(value, summed):
    devices = lax.axis_size("rows")
    if devices & (devices - 1):
        return [lax.psum(value, "rows"), jnp.zeros_like(value)]
    bits = [1 << k for k in range(devices.bit_length() - 1)]
    stages = [bits[:1]]
    if len(bits) > 2:
        stages.append([bits[1], bits[2], bits[1] + bits[2]])
        bits = bits[3:]
    else:
        bits = bits[1:]
    stages.extend([bit] for bit in bits)
    terms = [value]
    for stage in stages:
        if len(terms) > 1:
            terms = [summed(terms)]
        terms.extend([
            lax.ppermute(terms[0], "rows", [(i, i ^ offset) for i in range(devices)])
            for offset in stage
        ])
    return terms


def local(positions, momenta, kick_strength, coupling, tangent, log_growth):
    rows, columns = positions.shape
    vectors = tangent.shape[3]
    devices = lax.axis_size("rows")
    groups = columns // LANES
    in_hbm = pl.BlockSpec(memory_space=pltpu.HBM)
    resident = pl.BlockSpec(memory_space=pltpu.VMEM)
    f32 = lambda *shape: pltpu.VMEM(shape, jnp.float32)
    bf16 = lambda *shape: pltpu.VMEM(shape, jnp.bfloat16)
    near_core = lambda array: pltpu.with_memory_space_constraint(array, pltpu.VMEM)
    tangent = pltpu.with_memory_space_constraint(tangent, pltpu.HBM)

    tail_sites = columns // 4 if columns % (4 * LANES) == 0 else LANES
    head = columns - tail_sites
    near, far, tail = pl.pallas_call(
        edges_kernel,
        out_shape=[
            f32(columns + groups, vectors), f32(head + groups, vectors), f32(tail_sites, vectors)
        ],
        in_specs=[in_hbm, in_hbm],
        out_specs=[resident] * 3,
        scratch_shapes=[
            pltpu.VMEM((rows, columns), jnp.float32), pltpu.SemaphoreType.DMA((4,))
        ],
        compiler_params=pltpu.CompilerParams(vmem_limit_bytes=4 * MIB),
        name="edges",
    )(tangent, pltpu.with_memory_space_constraint(positions, pltpu.HBM))
    outward = [(i, (i + 1 if i % 2 else i - 1) % devices) for i in range(devices)]
    far = lax.ppermute(far, "rows", outward)
    near = lax.ppermute(near, "rows", [(i, i ^ 1) for i in range(devices)])
    tail = lax.ppermute(tail, "rows", outward)

    inner_pairs, partial, inner_gram = pl.pallas_call(
        inner_kernel,
        out_shape=[
            bf16(2, rows - 2, columns, 2 * vectors),
            f32(2, 2, columns, vectors),
            f32(vectors, vectors),
        ],
        in_specs=[in_hbm, resident, resident, resident],
        out_specs=[resident] * 3,
        scratch_shapes=[
            pltpu.VMEM((rows, columns + 16, vectors), jnp.float32),
            pltpu.VMEM((rows, columns, vectors), jnp.float32),
            pltpu.VMEM((rows, LANES, LANES), jnp.float32),
            pltpu.SemaphoreType.DMA((2, rows)),
        ],
        compiler_params=pltpu.CompilerParams(vmem_limit_bytes=16 * MIB),
        cost_estimate=pl.CostEstimate(
            flops=2 * 10**9, bytes_accessed=8 * MIB, transcendentals=0
        ),
        name="inner",
    )(tangent, positions, kick_strength, coupling)

    def finish(name, side, sites, halo, before):
        return pl.pallas_call(
            functools.partial(row_gram_kernel, side),
            out_shape=[
                bf16(2, sites, 2 * vectors), f32(vectors, vectors), f32(LANES, LANES)
            ],
            in_specs=[resident] * 5,
            out_specs=[resident] * 3,
            scratch_shapes=[pltpu.VMEM((LANES, LANES), jnp.float32)],
            compiler_params=pltpu.CompilerParams(vmem_limit_bytes=8 * MIB),
            cost_estimate=pl.CostEstimate(
                flops=4 * 10**8, bytes_accessed=2 * MIB, transcendentals=0
            ),
            name=name,
        )(
            near_core(halo), near_core(partial), near_core(positions), near_core(coupling),
            near_core(before),
        )

    packed_rows = vectors // 2 + 8
    near_pairs, gram, _ = finish("near", 0, columns, near, inner_gram)
    far_pairs, gram, table = finish("far", 1, head, far, gram)
    tail_pairs, gram = pl.pallas_call(
        functools.partial(tail_gram_kernel, head),
        out_shape=[bf16(2, tail_sites, 2 * vectors), f32(packed_rows, vectors)],
        in_specs=[resident] * 4,
        out_specs=[resident] * 2,
        compiler_params=pltpu.CompilerParams(vmem_limit_bytes=8 * MIB),
        name="tail",
    )(near_core(tail), near_core(partial), near_core(table), near_core(gram))

    def summed(terms):
        return pl.pallas_call(
            add_kernel,
            out_shape=f32(packed_rows, vectors),
            in_specs=[resident] * len(terms),
            out_specs=resident,
            compiler_params=pltpu.CompilerParams(vmem_limit_bytes=1 * MIB),
            name="gram_sum",
        )(*[near_core(term) for term in terms])

    terms = sum_over_rows(gram, summed)
    if len(terms) > 2:
        terms = [summed(terms), jnp.zeros_like(gram)]
    gram, gram_other = terms

    new_positions, new_momenta = pl.pallas_call(
        functools.partial(angles_kernel, columns, head),
        out_shape=[jax.ShapeDtypeStruct((rows, columns), jnp.float32)] * 2,
        in_specs=[resident] * 6,
        out_specs=[resident] * 2,
        compiler_params=pltpu.CompilerParams(vmem_limit_bytes=4 * MIB),
        cost_estimate=pl.CostEstimate(flops=10**6, bytes_accessed=10**6, transcendentals=0),
        name="angles",
    )(near_core(near), near_core(far), positions, momenta, kick_strength, coupling)

    sites_total = rows * devices * columns
    tangent_out, growth = pl.pallas_call(
        functools.partial(ortho_kernel, sites_total),
        out_shape=[
            pltpu.HBM((2, rows, columns, vectors), jnp.float32),
            jax.ShapeDtypeStruct((1, vectors), jnp.float32),
        ],
        in_specs=[resident] * 7,
        out_specs=[in_hbm, resident],
        scratch_shapes=[
            pltpu.VMEM((2 * vectors, 2 * vectors), jnp.bfloat16),
            pltpu.VMEM((2, rows, columns, vectors), jnp.float32),
            pltpu.SemaphoreType.DMA((2, rows)),
        ],
        compiler_params=pltpu.CompilerParams(vmem_limit_bytes=16 * MIB),
        name="ortho",
    )(
        near_core(gram), near_core(gram_other), log_growth.reshape(1, vectors),
        near_core(inner_pairs), near_core(near_pairs), near_core(far_pairs), near_core(tail_pairs),
    )
    return (new_positions, new_momenta, tangent_out, growth.reshape(vectors))


def solution(mesh):
    placed = (
        P("rows", "groups"),
        P("rows", "groups"),
        P("rows", None),
        P("rows", None),
        P("groups", "rows", None, None),
        P("groups"),
    )
    return jax.shard_map(
        local,
        mesh=mesh,
        in_specs=placed,
        out_specs=(
            P("rows", "groups"),
            P("rows", "groups"),
            P("groups", "rows", None, None),
            P("groups"),
        ),
        check_vma=False,
    )
```

```python
import functools
import math

import jax
import jax.numpy as jnp
from jax import lax
from jax.experimental import pallas as pl
from jax.experimental.pallas import tpu as pltpu
from jax.sharding import PartitionSpec as P

LANES = 128
MIB = 1 << 20


def lane_roll(field, shift):
    return pltpu.roll(field, shift % field.shape[1], axis=1)


def split_pair(value):
    high = value.astype(jnp.bfloat16)
    low = (value - high.astype(jnp.float32)).astype(jnp.bfloat16)
    return jnp.concatenate([high, low], axis=1)


def pair_gram(pairs):
    return lax.dot_general(
        pairs, pairs, (((0,), (0,)), ((), ())), preferred_element_type=jnp.float32
    )


def fold_pairs(gram):
    half = gram.shape[0] // 2
    return (gram[:half, :half] + gram[half:, half:]) + (gram[:half, half:] + gram[half:, :half])


def edge_kernel(side, earlier, tangent_ref, positions_hbm, *refs):
    first_ref, second_ref, positions_ref, sems = refs[earlier:]
    rows, columns = positions_ref.shape
    head = columns - second_ref.shape[0]
    row = side_slot(side) * (rows - 1)
    source = tangent_ref.at[0, row]
    copies = [
        pltpu.make_async_copy(positions_hbm, positions_ref, sems.at[0]),
        pltpu.make_async_copy(source.at[pl.ds(0, head)], first_ref.at[pl.ds(0, head)], sems.at[1]),
        pltpu.make_async_copy(source.at[pl.ds(head, columns - head)], second_ref, sems.at[2]),
    ]
    for copy in copies:
        copy.start()
    copies[0].wait()
    angles = positions_ref[pl.ds(row, 1), :]
    for group in range(columns // LANES):
        first_ref[head + group : head + group + 1, :] = angles[
            :, group * LANES : (group + 1) * LANES
        ]
    for copy in copies[1:]:
        copy.wait()


def inner_kernel(
    tangent_ref, positions_ref, kick_ref, coupling_ref,
    pairs_ref, partial_ref, gram_ref,
    pos_pad, mom_buf, stack, sems,
):
    rows, columns = positions_ref.shape
    groups = columns // LANES
    order = [*range(rows)]
    pos_copies = [
        pltpu.make_async_copy(
            tangent_ref.at[0, r], pos_pad.at[r, pl.ds(8, columns)], sems.at[0, r]
        )
        for r in order
    ]
    mom_copies = [
        pltpu.make_async_copy(tangent_ref.at[1, r], mom_buf.at[r], sems.at[1, r]) for r in order
    ]
    for r in order:
        pos_copies[r].start()
        mom_copies[r].start()

    x = positions_ref[...]
    coupling = coupling_ref[...]
    left = coupling * jnp.cos(lane_roll(x, 1) - x)
    right = coupling * jnp.cos(lane_roll(x, -1) - x)
    vertical = jnp.cos(x[1:] - x[:-1])
    none = jnp.zeros((1, columns), jnp.float32)
    up = coupling * jnp.concatenate([none, vertical], axis=0)
    down = coupling * jnp.concatenate([vertical, none], axis=0)
    centre = kick_ref[...] * jnp.cos(x) - ((left + right) + (up + down))
    for k, weight in enumerate((centre, left, right, up, down)):
        for r in range(rows):
            for group in range(groups):
                at = k * groups + group
                stack[r, at : at + 1, :] = weight[r : r + 1, group * LANES : (group + 1) * LANES]

    for r in order:
        pos_copies[r].wait()
        mom_copies[r].wait()
        pos_pad[r, 7:8, :] = pos_pad[r, 7 + columns : 8 + columns, :]
        pos_pad[r, 8 + columns : 9 + columns, :] = pos_pad[r, 8:9, :]

    def stepped(r, group, table, sides):
        at = 8 + group * LANES
        factor = lambda k: jnp.broadcast_to(
            table[:, k * groups + group : k * groups + group + 1], (LANES, LANES)
        )
        u = pos_pad[r, at : at + LANES, :]
        total = mom_buf[r, group * LANES : (group + 1) * LANES, :] + factor(0) * u
        total = total + factor(1) * pos_pad[r, at - 1 : at - 1 + LANES, :]
        total = total + factor(2) * pos_pad[r, at + 1 : at + 1 + LANES, :]
        for k, other in sides:
            total = total + factor(k) * pos_pad[other, at : at + LANES, :]
        return u, total

    for slot, (r, sides) in enumerate(((0, ((4, 1),)), (rows - 1, ((3, rows - 2),)))):
        table = stack[r].T
        for group in range(groups):
            u, total = stepped(r, group, table, sides)
            partial_ref[0, slot, group * LANES : (group + 1) * LANES, :] = u
            partial_ref[1, slot, group * LANES : (group + 1) * LANES, :] = total

    gram = jnp.zeros((2 * LANES, 2 * LANES), jnp.float32)
    for r in range(1, rows - 1):
        table = stack[r].T
        for group in range(groups):
            u, mom = stepped(r, group, table, ((3, r - 1), (4, r + 1)))
            span = pl.ds(group * LANES, LANES)
            pairs_ref[0, r - 1, span, :] = split_pair(u + mom)
            pairs_ref[1, r - 1, span, :] = split_pair(mom)
        for part in range(2):
            gram = gram + pair_gram(pairs_ref[part, r - 1])
    gram_ref[...] = fold_pairs(gram)


def side_slot(side):
    odd = lax.rem(lax.axis_index("rows"), 2)
    return odd if side else 1 - odd


def pack_symmetric(gram):
    half = gram.shape[0] // 2
    shape = (half, 2 * half)
    row = lax.broadcasted_iota(jnp.int32, shape, 0)
    lane = lax.broadcasted_iota(jnp.int32, shape, 1)
    corner = lane_roll(gram[half:], half)
    top = jnp.where((lane < half) & (lane > row), corner, gram[:half])
    diagonal = jnp.sum(jnp.where(lane == row, corner, 0.0), axis=0, keepdims=True)
    return jnp.concatenate([top, jnp.broadcast_to(diagonal, (8, 2 * half))], axis=0)


def unpack_symmetric(packed):
    order = packed.shape[1]
    half = order // 2
    top = packed[:half]
    row = lax.broadcasted_iota(jnp.int32, (half, order), 0)
    lane = lax.broadcasted_iota(jnp.int32, (half, order), 1)
    on = lane == row
    upper = jnp.where((lane >= half) | (lane < row), top, jnp.where(on, 0.5 * top, 0.0))
    corner = jnp.where(
        (lane < half) & (lane > row), top, jnp.where(on, 0.5 * packed[half : half + 1], 0.0)
    )
    triangle = jnp.concatenate([upper, lane_roll(corner, half)], axis=0)
    return triangle + triangle.T


def finish_sites(table, first_group, first, slot, halo, partial_ref, pairs_ref):
    for group in range(pairs_ref.shape[1] // LANES):
        span = slice(group * LANES, (group + 1) * LANES)
        from_first = slice(first + group * LANES, first + (group + 1) * LANES)
        at = first_group + group
        factor = jnp.broadcast_to(table[:, at : at + 1], (LANES, LANES))
        u = partial_ref[0, slot, from_first, :]
        mom = partial_ref[1, slot, from_first, :] + factor * (halo(group * LANES) - u)
        pairs_ref[0, span, :] = split_pair(u + mom)
        pairs_ref[1, span, :] = split_pair(mom)
    return fold_pairs(pair_gram(pairs_ref[0]) + pair_gram(pairs_ref[1]))


def row_gram_kernel(
    side, parts, *refs,
):
    halo_ref, halo_rest = refs[0], refs[1:parts]
    (
        partial_ref, positions_ref, coupling_ref, before_ref, pairs_ref, gram_ref, *table_ref, stack
    ) = refs[parts:]
    columns = positions_ref.shape[1]
    sites = halo_ref.shape[0] - columns // LANES

    def halo(at):
        if at < sites:
            return halo_ref[at : at + LANES, :]
        return halo_rest[0][at - sites : at - sites + LANES, :]

    slot = side_slot(side)
    row = slot * (positions_ref.shape[0] - 1)
    x = positions_ref[pl.ds(row, 1), :]
    coupling = coupling_ref[pl.ds(row, 1), :]
    for group in range(columns // LANES):
        span = slice(group * LANES, (group + 1) * LANES)
        stack[group : group + 1, :] = coupling[:, span] * jnp.cos(
            halo_ref[sites + group : sites + group + 1, :] - x[:, span]
        )
    table = stack[...].T
    if table_ref:
        table_ref[0][...] = table
    gram = finish_sites(table, 0, 0, slot, halo, partial_ref, pairs_ref)
    gram_ref[...] = before_ref[...] + gram


def tail_gram_kernel(first, halo_ref, partial_ref, table_ref, before_ref, pairs_ref, packed_ref):
    gram = finish_sites(
        table_ref[...], first // LANES, first, side_slot(1),
        lambda at: halo_ref[at : at + LANES, :], partial_ref, pairs_ref,
    )
    packed_ref[...] = pack_symmetric(before_ref[...] + gram)


def pairwise(terms):
    while len(terms) > 1:
        terms = [
            terms[i] + terms[i + 1] if i + 1 < len(terms) else terms[i]
            for i in range(0, len(terms), 2)
        ]
    return terms[0]


def add_kernel(*refs):
    refs[-1][...] = pairwise([ref[...] for ref in refs[:-1]])


def angles_kernel(
    near_at, far_at, near_ref, far_ref, positions_ref, momenta_ref, kick_ref, coupling_ref,
    new_positions_ref, new_momenta_ref,
):
    rows, columns = positions_ref.shape
    odd = lax.rem(lax.axis_index("rows"), 2) == 1
    lay = lambda ref, at: jnp.concatenate(
        [ref[at + g : at + g + 1, :] for g in range(columns // LANES)], axis=1
    )
    near, far = lay(near_ref, near_at), lay(far_ref, far_at)
    x = positions_ref[...]
    above = jnp.concatenate([jnp.where(odd, near, far), x[:-1]], axis=0)
    below = jnp.concatenate([x[1:], jnp.where(odd, far, near)], axis=0)
    spring = jnp.sin(above - x) + jnp.sin(below - x)
    spring = spring + jnp.sin(lane_roll(x, 1) - x)
    spring = spring + jnp.sin(lane_roll(x, -1) - x)
    momenta = momenta_ref[...] + kick_ref[...] * jnp.sin(x) + coupling_ref[...] * spring
    new_momenta_ref[...] = momenta
    new_positions_ref[...] = x + momenta


def three(value):
    first = value.astype(jnp.bfloat16).astype(jnp.float32)
    rest = value - first
    second = rest.astype(jnp.bfloat16).astype(jnp.float32)
    return first, second, (rest - second).astype(jnp.bfloat16).astype(jnp.float32)


def inverse_factor(gram, scale, weights_ref):
    order = gram.shape[0]
    step = 8
    lane = lax.broadcasted_iota(jnp.int32, (step, order), 1)
    sub = lax.broadcasted_iota(jnp.int32, (step, order), 0)
    spread = lambda value: jnp.broadcast_to(value, (step, order))
    work = [gram[at : at + step, :] for at in range(0, order, step)]
    squares = jnp.ones((step, order), jnp.float32)
    inverse = []
    for block in range(order // step):
        first = block * step
        own = work[block]
        if block == 0:
            columns = [spread(own[:, first + a : first + a + 1]) for a in range(step)]
        pivot = [
            [spread(columns[a][i : i + 1, :]) if i >= a else None for a in range(step)]
            for i in range(step)
        ]
        inside = (lane >= first) & (lane < first + step)
        extended = jnp.where(inside, jnp.where(lane - first == sub, 1.0, 0.0), own)
        solved = [spread(extended[a : a + 1, :]) for a in range(step)]
        recip = [None] * step
        lower = [[None] * step for _ in range(step)]
        ahead = None
        if block + 1 < order // step:
            ahead = work[block + 1]
            ahead_columns = [spread(ahead[:, first + a : first + a + 1]) for a in range(step)]
            coming = [
                spread(ahead[:, first + step + b : first + step + b + 1]) for b in range(step)
            ]
            ahead = jnp.where(inside, 0.0, ahead)
        for a in range(step):
            recip[a] = 1.0 / pivot[a][a]
            for i in range(a + 1, step):
                lower[i][a] = pivot[i][a] * recip[a]
            for b in range(a + 1, step):
                for i in range(b, step):
                    pivot[i][b] = pivot[i][b] - lower[i][a] * pivot[b][a]
            for i in range(a + 1, step):
                solved[i] = solved[i] - lower[i][a] * solved[a]
            if ahead is not None:
                factor = ahead_columns[a] * recip[a]
                ahead = ahead - factor * solved[a]
                for b in range(step):
                    coming[b] = coming[b] - factor * spread(ahead_columns[a][b : b + 1, :])
                for b in range(a + 1, step):
                    ahead_columns[b] = ahead_columns[b] - factor * pivot[b][a]
        if ahead is not None:
            work[block + 1], columns = ahead, coming
        scaled = [solved[a] * recip[a] for a in range(step)]
        for a in range(step - 1, 0, -1):
            for i in range(a):
                scaled[i] = scaled[i] - lower[a][i] * scaled[a]
        reach = min(block + 3, order // step)
        for later in range(block + 2, reach):
            rest = work[later]
            t = [spread(rest[:, first + a : first + a + 1]) * scaled[a] for a in range(step)]
            while len(t) > 1:
                t = [t[i] + t[i + 1] for i in range(0, len(t), 2)]
            work[later] = jnp.where(inside, 0.0, rest) - t[0]
        if reach < order // step:
            rows_y, rows_s = solved[0], solved[0] * recip[0]
            for a in range(1, step):
                rows_y = jnp.where(sub == a, solved[a], rows_y)
                rows_s = jnp.where(sub == a, solved[a] * recip[a], rows_s)
            y1, y2, y3 = three(rows_y)
            s1, s2, s3 = three(rows_s)
            left = jnp.concatenate([y1, y1, y2, y1, y3, y2], axis=0).astype(jnp.bfloat16)
            right = jnp.concatenate([s1, s2, s1, s3, s1, s2], axis=0).astype(jnp.bfloat16)
            update = lax.dot_general(
                left, right, (((0,), (0,)), ((), ())), preferred_element_type=jnp.float32
            )
            for later in range(reach, order // step):
                work[later] = jnp.where(inside, 0.0, work[later]) - update[
                    later * step : (later + 1) * step, :
                ]
        rows_out, diagonal = solved[0], pivot[0][0]
        for a in range(step):
            rows_out = jnp.where(sub == a, solved[a], rows_out)
            diagonal = jnp.where(sub == a, pivot[a][a], diagonal)
            squares = jnp.where(lane == first + a, pivot[a][a], squares)
        inverse.append(jnp.where(
            lane <= first + sub, rows_out * (scale * lax.rsqrt(diagonal)), 0.0
        ))
        if block % 2:
            factor = split_pair(jnp.concatenate(inverse[-2:], axis=0))
            high, low = factor[:, :order], factor[:, order:]
            at = first - step
            weights_ref[at : at + 2 * step, :] = jnp.concatenate([high, high], axis=1)
            weights_ref[order + at : order + at + 2 * step, :] = jnp.concatenate([low, low], axis=1)
    return squares


def ortho_kernel(
    sites_total, gram_ref, other_ref, log_growth_ref, inner_ref, near_ref, far_ref, tail_ref,
    out_ref, growth_ref,
    weights_ref, out_buf, out_sems,
):
    rows, columns = out_ref.shape[1], out_ref.shape[2]
    head = far_ref.shape[1]
    squares = inverse_factor(
        unpack_symmetric(gram_ref[...] + other_ref[...]), math.sqrt(sites_total), weights_ref
    )
    growth_ref[...] = (
        log_growth_ref[...] + 0.5 * jnp.log(squares[:1]) - 0.5 * math.log(sites_total)
    )
    weights = weights_ref[...]

    def product(pairs):
        both = lax.dot_general(
            pairs, weights, (((1,), (1,)), ((), ())), preferred_element_type=jnp.float32
        )
        return both[:, :LANES] + both[:, LANES:]

    stores = []
    piece = columns - head

    def send(part, slot, row):
        store = pltpu.make_async_copy(
            out_buf.at[part, slot], out_ref.at[part, row], out_sems.at[part, slot]
        )
        store.start()
        stores.append(store)

    for part in range(2):
        for r in range(rows - 2):
            for at in range(0, columns, piece):
                out_buf[part, r, at : at + piece] = product(inner_ref[part, r, at : at + piece])
            send(part, r, r + 1)
        for at in range(0, columns, piece):
            out_buf[part, rows - 2, at : at + piece] = product(near_ref[part, at : at + piece])
        send(part, rows - 2, side_slot(0) * (rows - 1))
        for at in range(0, head, piece):
            out_buf[part, rows - 1, at : at + piece] = product(far_ref[part, at : at + piece])
        out_buf[part, rows - 1, head:] = product(tail_ref[part])
        send(part, rows - 1, side_slot(1) * (rows - 1))
    for store in stores:
        store.wait()


def sum_over_rows(value, summed):
    devices = lax.axis_size("rows")
    if devices & (devices - 1):
        return [lax.psum(value, "rows"), jnp.zeros_like(value)]
    bits = [1 << k for k in range(devices.bit_length() - 1)]
    stages = [bits[:1]]
    if len(bits) > 2:
        stages.append([bits[1], bits[2], bits[1] + bits[2]])
        bits = bits[3:]
    else:
        bits = bits[1:]
    stages.extend([bit] for bit in bits)
    terms = [value]
    for stage in stages:
        if len(terms) > 1:
            terms = [summed(terms)]
        terms.extend([
            lax.ppermute(terms[0], "rows", [(i, i ^ offset) for i in range(devices)])
            for offset in stage
        ])
    return terms


def local(positions, momenta, kick_strength, coupling, tangent, log_growth):
    rows, columns = positions.shape
    vectors = tangent.shape[3]
    devices = lax.axis_size("rows")
    groups = columns // LANES
    in_hbm = pl.BlockSpec(memory_space=pltpu.HBM)
    resident = pl.BlockSpec(memory_space=pltpu.VMEM)
    f32 = lambda *shape: pltpu.VMEM(shape, jnp.float32)
    bf16 = lambda *shape: pltpu.VMEM(shape, jnp.bfloat16)
    near_core = lambda array: pltpu.with_memory_space_constraint(array, pltpu.VMEM)
    tangent = pltpu.with_memory_space_constraint(tangent, pltpu.HBM)

    tail_sites = columns // 4 if columns % (4 * LANES) == 0 else LANES
    head = columns - tail_sites
    half = columns // 2

    def edge(name, side, first_sites, *earlier):
        return pl.pallas_call(
            functools.partial(edge_kernel, side, len(earlier)),
            out_shape=[
                f32(first_sites + groups, vectors), f32(columns - first_sites, vectors)
            ],
            in_specs=[in_hbm, in_hbm] + [resident] * len(earlier),
            out_specs=[resident] * 2,
            scratch_shapes=[
                pltpu.VMEM((rows, columns), jnp.float32), pltpu.SemaphoreType.DMA((3,))
            ],
            compiler_params=pltpu.CompilerParams(vmem_limit_bytes=4 * MIB),
            name=name,
        )(tangent, pltpu.with_memory_space_constraint(positions, pltpu.HBM), *earlier)

    far, tail = edge("far_edge", 1, head)
    packed = tail
    outward = [(i, (i + 1 if i % 2 else i - 1) % devices) for i in range(devices)]
    far = lax.ppermute(far, "rows", outward)
    near, rest = edge("near_edge", 0, half, near_core(packed))
    near = lax.ppermute(near, "rows", [(i, i ^ 1) for i in range(devices)])
    rest = lax.ppermute(rest, "rows", [(i, i ^ 1) for i in range(devices)])
    tail = lax.ppermute(tail, "rows", outward)

    inner_pairs, partial, inner_gram = pl.pallas_call(
        inner_kernel,
        out_shape=[
            bf16(2, rows - 2, columns, 2 * vectors),
            f32(2, 2, columns, vectors),
            f32(vectors, vectors),
        ],
        in_specs=[in_hbm, resident, resident, resident],
        out_specs=[resident] * 3,
        scratch_shapes=[
            pltpu.VMEM((rows, columns + 16, vectors), jnp.float32),
            pltpu.VMEM((rows, columns, vectors), jnp.float32),
            pltpu.VMEM((rows, LANES, LANES), jnp.float32),
            pltpu.SemaphoreType.DMA((2, rows)),
        ],
        compiler_params=pltpu.CompilerParams(vmem_limit_bytes=16 * MIB),
        cost_estimate=pl.CostEstimate(
            flops=2 * 10**9, bytes_accessed=8 * MIB, transcendentals=0
        ),
        name="inner",
    )(tangent, positions, kick_strength, coupling)

    def finish(name, side, sites, halos, before, tables):
        return pl.pallas_call(
            functools.partial(row_gram_kernel, side, len(halos)),
            out_shape=[
                bf16(2, sites, 2 * vectors), f32(vectors, vectors),
                *[f32(LANES, LANES)] * tables,
            ],
            in_specs=[resident] * (4 + len(halos)),
            out_specs=[resident] * (2 + tables),
            scratch_shapes=[pltpu.VMEM((LANES, LANES), jnp.float32)],
            compiler_params=pltpu.CompilerParams(vmem_limit_bytes=8 * MIB),
            cost_estimate=pl.CostEstimate(
                flops=4 * 10**8, bytes_accessed=2 * MIB, transcendentals=0
            ),
            name=name,
        )(
            *[near_core(halo) for halo in halos], near_core(partial), near_core(positions),
            near_core(coupling), near_core(before),
        )

    packed_rows = vectors // 2 + 8
    near_pairs, gram = finish("near", 0, columns, [near, rest], inner_gram, 0)
    far_pairs, gram, table = finish("far", 1, head, [far], gram, 1)
    tail_pairs, gram = pl.pallas_call(
        functools.partial(tail_gram_kernel, head),
        out_shape=[bf16(2, tail_sites, 2 * vectors), f32(packed_rows, vectors)],
        in_specs=[resident] * 4,
        out_specs=[resident] * 2,
        compiler_params=pltpu.CompilerParams(vmem_limit_bytes=8 * MIB),
        name="tail",
    )(near_core(tail), near_core(partial), near_core(table), near_core(gram))

    def summed(terms):
        return pl.pallas_call(
            add_kernel,
            out_shape=f32(packed_rows, vectors),
            in_specs=[resident] * len(terms),
            out_specs=resident,
            compiler_params=pltpu.CompilerParams(vmem_limit_bytes=1 * MIB),
            name="gram_sum",
        )(*[near_core(term) for term in terms])

    terms = sum_over_rows(gram, summed)
    if len(terms) > 2:
        terms = [summed(terms), jnp.zeros_like(gram)]
    gram, gram_other = terms

    new_positions, new_momenta = pl.pallas_call(
        functools.partial(angles_kernel, half, head),
        out_shape=[jax.ShapeDtypeStruct((rows, columns), jnp.float32)] * 2,
        in_specs=[resident] * 6,
        out_specs=[resident] * 2,
        compiler_params=pltpu.CompilerParams(vmem_limit_bytes=4 * MIB),
        cost_estimate=pl.CostEstimate(flops=10**6, bytes_accessed=10**6, transcendentals=0),
        name="angles",
    )(near_core(near), near_core(far), positions, momenta, kick_strength, coupling)

    sites_total = rows * devices * columns
    tangent_out, growth = pl.pallas_call(
        functools.partial(ortho_kernel, sites_total),
        out_shape=[
            pltpu.HBM((2, rows, columns, vectors), jnp.float32),
            jax.ShapeDtypeStruct((1, vectors), jnp.float32),
        ],
        in_specs=[resident] * 7,
        out_specs=[in_hbm, resident],
        scratch_shapes=[
            pltpu.VMEM((2 * vectors, 2 * vectors), jnp.bfloat16),
            pltpu.VMEM((2, rows, columns, vectors), jnp.float32),
            pltpu.SemaphoreType.DMA((2, rows)),
        ],
        compiler_params=pltpu.CompilerParams(vmem_limit_bytes=16 * MIB),
        name="ortho",
    )(
        near_core(gram), near_core(gram_other), log_growth.reshape(1, vectors),
        near_core(inner_pairs), near_core(near_pairs), near_core(far_pairs), near_core(tail_pairs),
    )
    return (new_positions, new_momenta, tangent_out, growth.reshape(vectors))


def solution(mesh):
    placed = (
        P("rows", "groups"),
        P("rows", "groups"),
        P("rows", None),
        P("rows", None),
        P("groups", "rows", None, None),
        P("groups"),
    )
    return jax.shard_map(
        local,
        mesh=mesh,
        in_specs=placed,
        out_specs=(
            P("rows", "groups"),
            P("rows", "groups"),
            P("groups", "rows", None, None),
            P("groups"),
        ),
        check_vma=False,
    )
```

```python
import functools
import math

import jax
import jax.numpy as jnp
from jax import lax
from jax.experimental import pallas as pl
from jax.experimental.pallas import tpu as pltpu
from jax.sharding import PartitionSpec as P

LANES = 128
MIB = 1 << 20


def lane_roll(field, shift):
    return pltpu.roll(field, shift % field.shape[1], axis=1)


def split_pair(value):
    high = value.astype(jnp.bfloat16)
    low = (value - high.astype(jnp.float32)).astype(jnp.bfloat16)
    return jnp.concatenate([high, low], axis=1)


def pair_gram(pairs):
    return lax.dot_general(
        pairs, pairs, (((0,), (0,)), ((), ())), preferred_element_type=jnp.float32
    )


def fold_pairs(gram):
    half = gram.shape[0] // 2
    return (gram[:half, :half] + gram[half:, half:]) + (gram[:half, half:] + gram[half:, :half])


def edge_kernel(side, earlier, tangent_ref, positions_hbm, *refs):
    first_ref, second_ref, positions_ref, sems = refs[earlier:]
    rows, columns = positions_ref.shape
    head = columns - second_ref.shape[0]
    row = side_slot(side) * (rows - 1)
    source = tangent_ref.at[0, row]
    copies = [
        pltpu.make_async_copy(positions_hbm, positions_ref, sems.at[0]),
        pltpu.make_async_copy(source.at[pl.ds(0, head)], first_ref.at[pl.ds(0, head)], sems.at[1]),
        pltpu.make_async_copy(source.at[pl.ds(head, columns - head)], second_ref, sems.at[2]),
    ]
    for copy in copies:
        copy.start()
    copies[0].wait()
    angles = positions_ref[pl.ds(row, 1), :]
    for group in range(columns // LANES):
        first_ref[head + group : head + group + 1, :] = angles[
            :, group * LANES : (group + 1) * LANES
        ]
    for copy in copies[1:]:
        copy.wait()


def inner_kernel(
    tangent_ref, positions_ref, kick_ref, coupling_ref,
    pairs_ref, partial_ref, gram_ref,
    pos_pad, mom_buf, stack, sems,
):
    rows, columns = positions_ref.shape
    groups = columns // LANES
    order = [*range(rows)]
    pos_copies = [
        pltpu.make_async_copy(
            tangent_ref.at[0, r], pos_pad.at[r, pl.ds(8, columns)], sems.at[0, r]
        )
        for r in order
    ]
    mom_copies = [
        pltpu.make_async_copy(tangent_ref.at[1, r], mom_buf.at[r], sems.at[1, r]) for r in order
    ]
    for r in order:
        pos_copies[r].start()
        mom_copies[r].start()

    x = positions_ref[...]
    coupling = coupling_ref[...]
    left = coupling * jnp.cos(lane_roll(x, 1) - x)
    right = coupling * jnp.cos(lane_roll(x, -1) - x)
    vertical = jnp.cos(x[1:] - x[:-1])
    none = jnp.zeros((1, columns), jnp.float32)
    up = coupling * jnp.concatenate([none, vertical], axis=0)
    down = coupling * jnp.concatenate([vertical, none], axis=0)
    centre = kick_ref[...] * jnp.cos(x) - ((left + right) + (up + down))
    for k, weight in enumerate((centre, left, right, up, down)):
        for r in range(rows):
            for group in range(groups):
                at = k * groups + group
                stack[r, at : at + 1, :] = weight[r : r + 1, group * LANES : (group + 1) * LANES]

    for r in order:
        pos_copies[r].wait()
        mom_copies[r].wait()
        pos_pad[r, 7:8, :] = pos_pad[r, 7 + columns : 8 + columns, :]
        pos_pad[r, 8 + columns : 9 + columns, :] = pos_pad[r, 8:9, :]

    def stepped(r, group, table, sides):
        at = 8 + group * LANES
        factor = lambda k: jnp.broadcast_to(
            table[:, k * groups + group : k * groups + group + 1], (LANES, LANES)
        )
        u = pos_pad[r, at : at + LANES, :]
        total = mom_buf[r, group * LANES : (group + 1) * LANES, :] + factor(0) * u
        total = total + factor(1) * pos_pad[r, at - 1 : at - 1 + LANES, :]
        total = total + factor(2) * pos_pad[r, at + 1 : at + 1 + LANES, :]
        for k, other in sides:
            total = total + factor(k) * pos_pad[other, at : at + LANES, :]
        return u, total

    for slot, (r, sides) in enumerate(((0, ((4, 1),)), (rows - 1, ((3, rows - 2),)))):
        table = stack[r].T
        for group in range(groups):
            u, total = stepped(r, group, table, sides)
            partial_ref[0, slot, group * LANES : (group + 1) * LANES, :] = u
            partial_ref[1, slot, group * LANES : (group + 1) * LANES, :] = total

    gram = jnp.zeros((2 * LANES, 2 * LANES), jnp.float32)
    for r in range(1, rows - 1):
        table = stack[r].T
        for group in range(groups):
            u, mom = stepped(r, group, table, ((3, r - 1), (4, r + 1)))
            span = pl.ds(group * LANES, LANES)
            pairs_ref[0, r - 1, span, :] = split_pair(u + mom)
            pairs_ref[1, r - 1, span, :] = split_pair(mom)
        for part in range(2):
            gram = gram + pair_gram(pairs_ref[part, r - 1])
    gram_ref[...] = fold_pairs(gram)


def side_slot(side):
    odd = lax.rem(lax.axis_index("rows"), 2)
    return odd if side else 1 - odd


def pack_symmetric(gram):
    half = gram.shape[0] // 2
    shape = (half, 2 * half)
    row = lax.broadcasted_iota(jnp.int32, shape, 0)
    lane = lax.broadcasted_iota(jnp.int32, shape, 1)
    corner = lane_roll(gram[half:], half)
    top = jnp.where((lane < half) & (lane > row), corner, gram[:half])
    diagonal = jnp.sum(jnp.where(lane == row, corner, 0.0), axis=0, keepdims=True)
    return jnp.concatenate([top, jnp.broadcast_to(diagonal, (8, 2 * half))], axis=0)


def unpack_symmetric(packed):
    order = packed.shape[1]
    half = order // 2
    top = packed[:half]
    row = lax.broadcasted_iota(jnp.int32, (half, order), 0)
    lane = lax.broadcasted_iota(jnp.int32, (half, order), 1)
    on = lane == row
    upper = jnp.where((lane >= half) | (lane < row), top, jnp.where(on, 0.5 * top, 0.0))
    corner = jnp.where(
        (lane < half) & (lane > row), top, jnp.where(on, 0.5 * packed[half : half + 1], 0.0)
    )
    triangle = jnp.concatenate([upper, lane_roll(corner, half)], axis=0)
    return triangle + triangle.T


def finish_sites(table, first_group, first, slot, halo, partial_ref, pairs_ref):
    for group in range(pairs_ref.shape[1] // LANES):
        span = slice(group * LANES, (group + 1) * LANES)
        from_first = slice(first + group * LANES, first + (group + 1) * LANES)
        at = first_group + group
        factor = jnp.broadcast_to(table[:, at : at + 1], (LANES, LANES))
        u = partial_ref[0, slot, from_first, :]
        mom = partial_ref[1, slot, from_first, :] + factor * (halo(group * LANES) - u)
        pairs_ref[0, span, :] = split_pair(u + mom)
        pairs_ref[1, span, :] = split_pair(mom)
    return fold_pairs(pair_gram(pairs_ref[0]) + pair_gram(pairs_ref[1]))


def row_gram_kernel(
    side, parts, *refs,
):
    halo_ref, halo_rest = refs[0], refs[1:parts]
    (
        partial_ref, positions_ref, coupling_ref, before_ref, pairs_ref, gram_ref, *table_ref, stack
    ) = refs[parts:]
    columns = positions_ref.shape[1]
    sites = halo_ref.shape[0] - columns // LANES

    def halo(at):
        if at < sites:
            return halo_ref[at : at + LANES, :]
        return halo_rest[0][at - sites : at - sites + LANES, :]

    slot = side_slot(side)
    row = slot * (positions_ref.shape[0] - 1)
    x = positions_ref[pl.ds(row, 1), :]
    coupling = coupling_ref[pl.ds(row, 1), :]
    for group in range(columns // LANES):
        span = slice(group * LANES, (group + 1) * LANES)
        stack[group : group + 1, :] = coupling[:, span] * jnp.cos(
            halo_ref[sites + group : sites + group + 1, :] - x[:, span]
        )
    table = stack[...].T
    if table_ref:
        table_ref[0][...] = table
    gram = finish_sites(table, 0, 0, slot, halo, partial_ref, pairs_ref)
    gram_ref[...] = before_ref[...] + gram


def tail_gram_kernel(first, halo_ref, partial_ref, table_ref, before_ref, pairs_ref, packed_ref):
    gram = finish_sites(
        table_ref[...], first // LANES, first, side_slot(1),
        lambda at: halo_ref[at : at + LANES, :], partial_ref, pairs_ref,
    )
    packed_ref[...] = pack_symmetric(before_ref[...] + gram)


def pairwise(terms):
    while len(terms) > 1:
        terms = [
            terms[i] + terms[i + 1] if i + 1 < len(terms) else terms[i]
            for i in range(0, len(terms), 2)
        ]
    return terms[0]


def add_kernel(*refs):
    refs[-1][...] = pairwise([ref[...] for ref in refs[:-1]])


def angles_kernel(
    near_at, far_at, near_ref, far_ref, positions_ref, momenta_ref, kick_ref, coupling_ref,
    new_positions_ref, new_momenta_ref,
):
    rows, columns = positions_ref.shape
    odd = lax.rem(lax.axis_index("rows"), 2) == 1
    lay = lambda ref, at: jnp.concatenate(
        [ref[at + g : at + g + 1, :] for g in range(columns // LANES)], axis=1
    )
    near, far = lay(near_ref, near_at), lay(far_ref, far_at)
    x = positions_ref[...]
    above = jnp.concatenate([jnp.where(odd, near, far), x[:-1]], axis=0)
    below = jnp.concatenate([x[1:], jnp.where(odd, far, near)], axis=0)
    spring = jnp.sin(above - x) + jnp.sin(below - x)
    spring = spring + jnp.sin(lane_roll(x, 1) - x)
    spring = spring + jnp.sin(lane_roll(x, -1) - x)
    momenta = momenta_ref[...] + kick_ref[...] * jnp.sin(x) + coupling_ref[...] * spring
    new_momenta_ref[...] = momenta
    new_positions_ref[...] = x + momenta


def three(value):
    first = value.astype(jnp.bfloat16).astype(jnp.float32)
    rest = value - first
    second = rest.astype(jnp.bfloat16).astype(jnp.float32)
    return first, second, (rest - second).astype(jnp.bfloat16).astype(jnp.float32)


def inverse_factor(gram, scale, weights_ref):
    order = gram.shape[0]
    step = 8
    lane = lax.broadcasted_iota(jnp.int32, (step, order), 1)
    sub = lax.broadcasted_iota(jnp.int32, (step, order), 0)
    spread = lambda value: jnp.broadcast_to(value, (step, order))
    work = [gram[at : at + step, :] for at in range(0, order, step)]
    squares = jnp.ones((step, order), jnp.float32)
    inverse = []
    for block in range(order // step):
        first = block * step
        own = work[block]
        if block == 0:
            columns = [spread(own[:, first + a : first + a + 1]) for a in range(step)]
        pivot = [
            [spread(columns[a][i : i + 1, :]) if i >= a else None for a in range(step)]
            for i in range(step)
        ]
        inside = (lane >= first) & (lane < first + step)
        extended = jnp.where(inside, jnp.where(lane - first == sub, 1.0, 0.0), own)
        solved = [spread(extended[a : a + 1, :]) for a in range(step)]
        recip = [None] * step
        lower = [[None] * step for _ in range(step)]
        ahead = None
        if block + 1 < order // step:
            ahead = work[block + 1]
            ahead_columns = [spread(ahead[:, first + a : first + a + 1]) for a in range(step)]
            coming = [
                spread(ahead[:, first + step + b : first + step + b + 1]) for b in range(step)
            ]
            ahead = jnp.where(inside, 0.0, ahead)
        for a in range(step):
            recip[a] = 1.0 / pivot[a][a]
            for i in range(a + 1, step):
                lower[i][a] = pivot[i][a] * recip[a]
            for b in range(a + 1, step):
                for i in range(b, step):
                    pivot[i][b] = pivot[i][b] - lower[i][a] * pivot[b][a]
            for i in range(a + 1, step):
                solved[i] = solved[i] - lower[i][a] * solved[a]
            if ahead is not None:
                factor = ahead_columns[a] * recip[a]
                ahead = ahead - factor * solved[a]
                for b in range(step):
                    coming[b] = coming[b] - factor * spread(ahead_columns[a][b : b + 1, :])
                for b in range(a + 1, step):
                    ahead_columns[b] = ahead_columns[b] - factor * pivot[b][a]
        if ahead is not None:
            work[block + 1], columns = ahead, coming
        scaled = [solved[a] * recip[a] for a in range(step)]
        for a in range(step - 1, 0, -1):
            for i in range(a):
                scaled[i] = scaled[i] - lower[a][i] * scaled[a]
        reach = min(block + 3, order // step)
        for later in range(block + 2, reach):
            rest = work[later]
            t = [spread(rest[:, first + a : first + a + 1]) * scaled[a] for a in range(step)]
            while len(t) > 1:
                t = [t[i] + t[i + 1] for i in range(0, len(t), 2)]
            work[later] = jnp.where(inside, 0.0, rest) - t[0]
        if reach < order // step:
            rows_y, rows_s = solved[0], solved[0] * recip[0]
            for a in range(1, step):
                rows_y = jnp.where(sub == a, solved[a], rows_y)
                rows_s = jnp.where(sub == a, solved[a] * recip[a], rows_s)
            y1, y2, y3 = three(rows_y)
            s1, s2, s3 = three(rows_s)
            left = jnp.concatenate([y1, y1, y2, y1, y3, y2], axis=0).astype(jnp.bfloat16)
            right = jnp.concatenate([s1, s2, s1, s3, s1, s2], axis=0).astype(jnp.bfloat16)
            update = lax.dot_general(
                left, right, (((0,), (0,)), ((), ())), preferred_element_type=jnp.float32
            )
            for later in range(reach, order // step):
                work[later] = jnp.where(inside, 0.0, work[later]) - update[
                    later * step : (later + 1) * step, :
                ]
        rows_out, diagonal = solved[0], pivot[0][0]
        for a in range(step):
            rows_out = jnp.where(sub == a, solved[a], rows_out)
            diagonal = jnp.where(sub == a, pivot[a][a], diagonal)
            squares = jnp.where(lane == first + a, pivot[a][a], squares)
        inverse.append(jnp.where(
            lane <= first + sub, rows_out * (scale * lax.rsqrt(diagonal)), 0.0
        ))
        if block % 2:
            factor = split_pair(jnp.concatenate(inverse[-2:], axis=0))
            high, low = factor[:, :order], factor[:, order:]
            at = first - step
            weights_ref[at : at + 2 * step, :] = jnp.concatenate([high, high], axis=1)
            weights_ref[order + at : order + at + 2 * step, :] = jnp.concatenate([low, low], axis=1)
    return squares


def ortho_kernel(
    sites_total, gram_ref, other_ref, log_growth_ref, inner_ref, near_ref, far_ref, tail_ref,
    out_ref, growth_ref,
    weights_ref, out_buf, out_sems,
):
    rows, columns = out_ref.shape[1], out_ref.shape[2]
    head = far_ref.shape[1]
    squares = inverse_factor(
        unpack_symmetric(gram_ref[...] + other_ref[...]), math.sqrt(sites_total), weights_ref
    )
    growth_ref[...] = (
        log_growth_ref[...] + 0.5 * jnp.log(squares[:1]) - 0.5 * math.log(sites_total)
    )
    weights = weights_ref[...]

    def product(pairs):
        both = lax.dot_general(
            pairs, weights, (((1,), (1,)), ((), ())), preferred_element_type=jnp.float32
        )
        return both[:, :LANES] + both[:, LANES:]

    stores = []
    piece = columns // 2

    def send(part, slot, row):
        store = pltpu.make_async_copy(
            out_buf.at[part, slot], out_ref.at[part, row], out_sems.at[part, slot]
        )
        store.start()
        stores.append(store)

    for part in range(2):
        for r in range(rows - 2):
            for at in range(0, columns, piece):
                out_buf[part, r, at : at + piece] = product(inner_ref[part, r, at : at + piece])
            send(part, r, r + 1)
        for at in range(0, columns, piece):
            out_buf[part, rows - 2, at : at + piece] = product(near_ref[part, at : at + piece])
        send(part, rows - 2, side_slot(0) * (rows - 1))
        for at in range(0, head, head // 2):
            out_buf[part, rows - 1, at : at + head // 2] = product(far_ref[part, at : at + head // 2])
        out_buf[part, rows - 1, head:] = product(tail_ref[part])
        send(part, rows - 1, side_slot(1) * (rows - 1))
    for store in stores:
        store.wait()


def sum_over_rows(value, summed):
    devices = lax.axis_size("rows")
    if devices & (devices - 1):
        return [lax.psum(value, "rows"), jnp.zeros_like(value)]
    bits = [1 << k for k in range(devices.bit_length() - 1)]
    stages = [bits[:1]]
    if len(bits) > 2:
        stages.append([bits[1], bits[2], bits[1] + bits[2]])
        bits = bits[3:]
    else:
        bits = bits[1:]
    stages.extend([bit] for bit in bits)
    terms = [value]
    for stage in stages:
        if len(terms) > 1:
            terms = [summed(terms)]
        terms.extend([
            lax.ppermute(terms[0], "rows", [(i, i ^ offset) for i in range(devices)])
            for offset in stage
        ])
    return terms


def local(positions, momenta, kick_strength, coupling, tangent, log_growth):
    rows, columns = positions.shape
    vectors = tangent.shape[3]
    devices = lax.axis_size("rows")
    groups = columns // LANES
    in_hbm = pl.BlockSpec(memory_space=pltpu.HBM)
    resident = pl.BlockSpec(memory_space=pltpu.VMEM)
    f32 = lambda *shape: pltpu.VMEM(shape, jnp.float32)
    bf16 = lambda *shape: pltpu.VMEM(shape, jnp.bfloat16)
    near_core = lambda array: pltpu.with_memory_space_constraint(array, pltpu.VMEM)
    tangent = pltpu.with_memory_space_constraint(tangent, pltpu.HBM)

    tail_sites = columns // 4 if columns % (4 * LANES) == 0 else LANES
    head = columns - tail_sites
    half = columns // 2

    def edge(name, side, first_sites, *earlier):
        return pl.pallas_call(
            functools.partial(edge_kernel, side, len(earlier)),
            out_shape=[
                f32(first_sites + groups, vectors), f32(columns - first_sites, vectors)
            ],
            in_specs=[in_hbm, in_hbm] + [resident] * len(earlier),
            out_specs=[resident] * 2,
            scratch_shapes=[
                pltpu.VMEM((rows, columns), jnp.float32), pltpu.SemaphoreType.DMA((3,))
            ],
            compiler_params=pltpu.CompilerParams(vmem_limit_bytes=4 * MIB),
            name=name,
        )(tangent, pltpu.with_memory_space_constraint(positions, pltpu.HBM), *earlier)

    far, tail = edge("far_edge", 1, head)
    packed = tail
    outward = [(i, (i + 1 if i % 2 else i - 1) % devices) for i in range(devices)]
    far = lax.ppermute(far, "rows", outward)
    near, rest = edge("near_edge", 0, half, near_core(packed))
    near = lax.ppermute(near, "rows", [(i, i ^ 1) for i in range(devices)])
    rest = lax.ppermute(rest, "rows", [(i, i ^ 1) for i in range(devices)])
    tail = lax.ppermute(tail, "rows", outward)

    inner_pairs, partial, inner_gram = pl.pallas_call(
        inner_kernel,
        out_shape=[
            bf16(2, rows - 2, columns, 2 * vectors),
            f32(2, 2, columns, vectors),
            f32(vectors, vectors),
        ],
        in_specs=[in_hbm, resident, resident, resident],
        out_specs=[resident] * 3,
        scratch_shapes=[
            pltpu.VMEM((rows, columns + 16, vectors), jnp.float32),
            pltpu.VMEM((rows, columns, vectors), jnp.float32),
            pltpu.VMEM((rows, LANES, LANES), jnp.float32),
            pltpu.SemaphoreType.DMA((2, rows)),
        ],
        compiler_params=pltpu.CompilerParams(vmem_limit_bytes=16 * MIB),
        cost_estimate=pl.CostEstimate(
            flops=2 * 10**9, bytes_accessed=8 * MIB, transcendentals=0
        ),
        name="inner",
    )(tangent, positions, kick_strength, coupling)

    def finish(name, side, sites, halos, before, tables):
        return pl.pallas_call(
            functools.partial(row_gram_kernel, side, len(halos)),
            out_shape=[
                bf16(2, sites, 2 * vectors), f32(vectors, vectors),
                *[f32(LANES, LANES)] * tables,
            ],
            in_specs=[resident] * (4 + len(halos)),
            out_specs=[resident] * (2 + tables),
            scratch_shapes=[pltpu.VMEM((LANES, LANES), jnp.float32)],
            compiler_params=pltpu.CompilerParams(vmem_limit_bytes=8 * MIB),
            cost_estimate=pl.CostEstimate(
                flops=4 * 10**8, bytes_accessed=2 * MIB, transcendentals=0
            ),
            name=name,
        )(
            *[near_core(halo) for halo in halos], near_core(partial), near_core(positions),
            near_core(coupling), near_core(before),
        )

    packed_rows = vectors // 2 + 8
    near_pairs, gram = finish("near", 0, columns, [near, rest], inner_gram, 0)
    far_pairs, gram, table = finish("far", 1, head, [far], gram, 1)
    tail_pairs, gram = pl.pallas_call(
        functools.partial(tail_gram_kernel, head),
        out_shape=[bf16(2, tail_sites, 2 * vectors), f32(packed_rows, vectors)],
        in_specs=[resident] * 4,
        out_specs=[resident] * 2,
        compiler_params=pltpu.CompilerParams(vmem_limit_bytes=8 * MIB),
        name="tail",
    )(near_core(tail), near_core(partial), near_core(table), near_core(gram))

    def summed(terms):
        return pl.pallas_call(
            add_kernel,
            out_shape=f32(packed_rows, vectors),
            in_specs=[resident] * len(terms),
            out_specs=resident,
            compiler_params=pltpu.CompilerParams(vmem_limit_bytes=1 * MIB),
            name="gram_sum",
        )(*[near_core(term) for term in terms])

    terms = sum_over_rows(gram, summed)
    if len(terms) > 2:
        terms = [summed(terms), jnp.zeros_like(gram)]
    gram, gram_other = terms

    new_positions, new_momenta = pl.pallas_call(
        functools.partial(angles_kernel, half, head),
        out_shape=[jax.ShapeDtypeStruct((rows, columns), jnp.float32)] * 2,
        in_specs=[resident] * 6,
        out_specs=[resident] * 2,
        compiler_params=pltpu.CompilerParams(vmem_limit_bytes=4 * MIB),
        cost_estimate=pl.CostEstimate(flops=10**6, bytes_accessed=10**6, transcendentals=0),
        name="angles",
    )(near_core(near), near_core(far), positions, momenta, kick_strength, coupling)

    sites_total = rows * devices * columns
    tangent_out, growth = pl.pallas_call(
        functools.partial(ortho_kernel, sites_total),
        out_shape=[
            pltpu.HBM((2, rows, columns, vectors), jnp.float32),
            jax.ShapeDtypeStruct((1, vectors), jnp.float32),
        ],
        in_specs=[resident] * 7,
        out_specs=[in_hbm, resident],
        scratch_shapes=[
            pltpu.VMEM((2 * vectors, 2 * vectors), jnp.bfloat16),
            pltpu.VMEM((2, rows, columns, vectors), jnp.float32),
            pltpu.SemaphoreType.DMA((2, rows)),
        ],
        compiler_params=pltpu.CompilerParams(vmem_limit_bytes=16 * MIB),
        name="ortho",
    )(
        near_core(gram), near_core(gram_other), log_growth.reshape(1, vectors),
        near_core(inner_pairs), near_core(near_pairs), near_core(far_pairs), near_core(tail_pairs),
    )
    return (new_positions, new_momenta, tangent_out, growth.reshape(vectors))


def solution(mesh):
    placed = (
        P("rows", "groups"),
        P("rows", "groups"),
        P("rows", None),
        P("rows", None),
        P("groups", "rows", None, None),
        P("groups"),
    )
    return jax.shard_map(
        local,
        mesh=mesh,
        in_specs=placed,
        out_specs=(
            P("rows", "groups"),
            P("rows", "groups"),
            P("groups", "rows", None, None),
            P("groups"),
        ),
        check_vma=False,
    )
```
